32 devices in a mesh: space: 16 (over z, y, core), snap: 2 (over x).
Axes of the slice: x: 2, y: 2, z: 4, core: 2. Of those that a mesh axis runs over, the one named last changes fastest.
Arguments:
- snaps_primal: bfloat16 [512, 49152], P('snap', 'space'), may hold values from -6 to 6
- snaps_adjoint: bfloat16 [512, 49152], P('snap', 'space'), may hold values from -6 to 6
- coef_primal: bfloat16 [512, 256], P('snap'), may hold values from -0.375 to 0.375
- coef_adjoint: bfloat16 [512, 256], P('snap'), may hold values from -0.375 to 0.375
- op_blocks: bfloat16 [384, 5, 128, 128], P('space'), may hold values from -0.25 to 0.25
- counts: int32 [384], P('space'), may hold values from 1 to 5, as said below
- col_index: int32 [384, 5], P('space'), may hold values from 0 to 47, as said below
- ghost_send: int32 [16, 4, 6], P('space'), may hold values from 0 to 23, as said below
Outputs:
- primal_modes: bfloat16 [256, 49152], P('snap', 'space')
- applied: bfloat16 [256, 49152], P('snap', 'space')
- reduced_operator: float32 [256, 256], P(None, 'snap')
- cross_gram: float32 [256, 256], P(None, 'snap')
The draws below stay inside these ranges and needn't reach their ends.
Inputs may be any that keep to these rules, and one draw needn't show every extreme that they name: `counts`: every block row has its slot 0 live. `col_index`: slot 0 of every block row names the row's own diagonal block; ghost entries never name a partition outside 0 to 15. `ghost_send`: the 6 entries of one list are distinct.
All inputs are finite; a program needn't handle non-finite values.
Results may differ from the reference program's by a relative error of at most 0.02.
Values may be sent and summed in bfloat16 or wider, within the bound.
A program may use at most 64 MiB of HBM per device.

```python
import math
import jax
import jax.numpy as jnp
from jax import lax

R = 256
BS = 128
NBL = 24
KMAX = 5
GH = 6
M = 512
NPART = 16
NSP = 49152
NBT = 384
N_SNAP = 2


def draw_counts(key, part):
    values = jax.random.randint(key, (NBT,), 1, KMAX + 1)
    rows = jnp.arange(NBT, dtype=jnp.int32)
    values = jnp.where(rows % NBL == 0, jnp.maximum(values, 3), values)
    values = values.at[0].set(KMAX).at[1].set(1)
    return values.astype(jnp.int32)


def draw_col_index(key, part):
    extent = NBL + 4 * GH
    slots = jax.random.randint(jax.random.fold_in(key, 7), (NBT, KMAX), 0, extent)
    rows = jnp.arange(NBT, dtype=jnp.int32)
    owner = rows // NBL
    direction = jnp.clip((slots - NBL) // GH, 0, 3)
    offsets = jnp.array([-2, -1, 1, 2], dtype=jnp.int32)
    source = owner[:, None] + offsets[direction]
    inside = (source >= 0) & (source < NPART)
    slots = jnp.where((slots >= NBL) & jnp.logical_not(inside), slots % NBL, slots)
    slots = slots.at[:, 0].set(rows % NBL)
    first_rows = (rows % NBL == 0) & (owner + 2 < NPART)
    slots = slots.at[:, 1].set(jnp.where(first_rows, extent - 1, slots[:, 1]))
    low_rows = (rows % NBL == 0) & (owner >= 2)
    slots = slots.at[:, 2].set(jnp.where(low_rows, NBL, slots[:, 2]))
    middle = NPART // 2 * NBL
    slots = slots.at[middle, 1].set(extent - 1)
    slots = slots.at[0, 1].set(NBL + 2 * GH).at[0, 2].set(NBL + 3 * GH)
    return slots.astype(jnp.int32)


def draw_ghost_send(key, part):
    keys = jax.random.split(jax.random.fold_in(key, 11), NPART * 4)
    lists = jax.vmap(lambda single: jax.random.permutation(single, NBL)[:GH])(keys)
    lists = lists.reshape(NPART, 4, GH)
    steps_up = jnp.arange(GH, dtype=jnp.int32)
    lists = lists.at[0, 0].set(steps_up).at[0, 1].set(NBL - 1 - steps_up)
    return lists.astype(jnp.int32)


def with_spikes(entries, key, source, target, shards_of, factor):
    def block_of(axis_at):
        return (jnp.arange(entries.shape[axis_at]) // (entries.shape[axis_at] // shards_of)).reshape((-1,) + (1,) * (entries.ndim - 1 - axis_at))

    first = jax.random.permutation(key, shards_of)[block_of(target)]
    other_side = (block_of(target) + shards_of // 2) % shards_of
    return jnp.where((block_of(source) == first) | (block_of(source) == other_side), factor * entries, entries)


def steps_of(key, shape, shards, least, high):
    def one(position, blocks):
        heights = jax.random.uniform(jax.random.fold_in(jax.random.fold_in(key, 6), position), (blocks,), jnp.float32, least / len(shards), high / len(shards))
        return jnp.repeat(jnp.exp(heights), shape[position] // blocks).reshape((-1,) + (1,) * (len(shape) - position - 1))

    level = one(*shards[0])
    for cut in shards[1:]:
        level = level * one(*cut)
    return level


def normal_values(stream_key, shape, deviation, reach, pieces=(), held_as=jnp.bfloat16):
    gain = steps_of(stream_key, shape, pieces, -0.22, 0.18) if pieces else 1.0
    values = jax.random.normal(stream_key, shape, jnp.float32) * deviation * gain
    return jnp.minimum(jnp.maximum(values, -reach), reach).astype(held_as)


def heavy_noise(rng, shape, scale, limit, cuts, heavy, held_as=jnp.bfloat16):
    drawn = scale * jax.random.normal(rng, shape, jnp.float32)
    if cuts:
        drawn = drawn * steps_of(rng, shape, cuts, -0.22, 0.18)
    return jnp.clip(with_spikes(drawn, jax.random.fold_in(rng, 3), *heavy), -limit, limit).astype(held_as)


def setup_inputs(seed: int = 0) -> dict:
    seeds = jax.random.split(jax.random.key(seed), 9)
    return {
        "snaps_primal": normal_values(seeds[0], (M, NSP), 1.0, 6.0, ((0, 2), (1, 16))),
        "snaps_adjoint": normal_values(seeds[1], (M, NSP), 1.0, 6.0, ((0, 2), (1, 16))),
        "coef_primal": heavy_noise(seeds[2], (M, R), M ** -0.5, 0.375, ((0, 2),), (0, 1, 2, 2.0)),
        "coef_adjoint": heavy_noise(seeds[3], (M, R), M ** -0.5, 0.375, ((0, 2),), (0, 1, 2, 2.0)),
        "op_blocks": normal_values(seeds[4], (NBT, KMAX, BS, BS), (BS * KMAX) ** -0.5, 0.25, ((0, 16),)),
        "counts": draw_counts(jax.random.fold_in(seeds[8], 71), 0),
        "col_index": draw_col_index(jax.random.fold_in(seeds[8], 71), 0),
        "ghost_send": draw_ghost_send(jax.random.fold_in(seeds[8], 71), 0),
    }


def make_modes(snaps, coef):
    width = M // N_SNAP
    total = jnp.zeros((R, NSP), jnp.float32)
    for group in range(N_SNAP):
        partial_term = jnp.dot(coef[group * width:(group + 1) * width].T, snaps[group * width:(group + 1) * width], preferred_element_type=jnp.float32)
        rounded = lax.optimization_barrier(partial_term.astype(jnp.bfloat16))
        total = total + rounded.astype(jnp.float32)
    return total.astype(jnp.bfloat16)

def reference(snaps_primal, snaps_adjoint, coef_primal, coef_adjoint, op_blocks, counts, col_index, ghost_send):
    primal = make_modes(snaps_primal, coef_primal)
    adjoint = make_modes(snaps_adjoint, coef_adjoint)
    rows = jnp.arange(NBT, dtype=jnp.int32)
    owner = rows // NBL
    ghost = col_index >= NBL
    direction = jnp.clip((col_index - NBL) // GH, 0, 3).astype(jnp.int32)
    entry = ((col_index - NBL) % GH).astype(jnp.int32)
    offsets = jnp.array([-2, -1, 1, 2], dtype=jnp.int32)
    source = jnp.clip(owner[:, None] + offsets[direction], 0, NPART - 1).astype(jnp.int32)
    remote = source * NBL + ghost_send[source, direction, entry]
    target = jnp.where(ghost, remote, owner[:, None] * NBL + col_index).astype(jnp.int32)
    live = (jnp.arange(KMAX, dtype=jnp.int32)[None, :] < counts[:, None]).astype(jnp.float32)
    blocks = primal.reshape(R, NBT, BS)

    def one_row(row):
        picked = blocks[:, target[row]].astype(jnp.float32) * live[row][None, :, None]
        mats = op_blocks[row].astype(jnp.float32)
        return jnp.einsum('mkc,kjc->mj', picked, mats)
    applied = lax.map(one_row, rows)
    applied = jnp.transpose(applied, (1, 0, 2)).reshape(R, NSP).astype(jnp.bfloat16)
    factor = 1.0 / math.sqrt(NSP)
    reduced = jnp.dot(adjoint, applied.T, preferred_element_type=jnp.float32) * factor
    gram = jnp.dot(adjoint, primal.T, preferred_element_type=jnp.float32) * factor
    return (primal, applied, reduced, gram)
```

```python
import math

import jax
import jax.numpy as jnp
from jax import lax
from jax.experimental import pallas as pl
from jax.experimental.pallas import tpu as pltpu
from jax.sharding import PartitionSpec as P

MESH = pl.DeviceIdType.MESH
BF16 = jnp.bfloat16
F32 = jnp.float32
OFFSETS = (-2, -1, 1, 2)
TILE_BLOCKS = 4
CHUNK = 64


class Sizes:
    def __init__(self, n_space, n_snap, snaps, coef, op_blocks, ghost_send):
        self.n_space, self.n_snap = n_space, n_snap
        self.devices = n_space * n_snap
        self.snaps, self.unknowns = snaps.shape
        self.modes = coef.shape[1]
        self.share = self.modes // n_snap
        self.rows, self.slots, self.bs = op_blocks.shape[:3]
        self.lists, self.list_len = ghost_send.shape[1:]
        self.mc = CHUNK
        self.chunks = self.modes // self.mc
        self.piece = max(16, self.modes // n_space)
        self.owners = self.modes // self.piece
        self.tiles = self.rows // TILE_BLOCKS
        self.factor = 1.0 / math.sqrt(self.unknowns * n_space)

    def groups(self, c):
        first, last = c * self.mc, (c + 1) * self.mc
        found = []
        for x in range(self.n_snap):
            lo, hi = max(first, x * self.share), min(last, (x + 1) * self.share)
            if lo < hi:
                found.append((x, lo - x * self.share, lo - first, hi - lo))
        return found


def scratch_of(z):
    b, mc, bs = z.rows, z.mc, z.bs
    one = {
        "q": pltpu.VMEM((b, mc, bs), BF16),
        "qr": pltpu.VMEM((z.n_snap - 1, b, mc, bs), BF16),
        "own": pltpu.VMEM((b, mc, bs), BF16),
        "ext": pltpu.VMEM((b + z.lists * z.list_len, mc, bs), BF16),
        "snd": pltpu.VMEM((z.lists, z.list_len, mc, bs), BF16),
        "st": pltpu.VMEM((b, 2 * mc, bs), BF16),
        "d": pltpu.VMEM((z.owners, z.piece, 2 * mc), BF16),
        "rs": pltpu.VMEM((z.devices, z.piece, 2 * mc), BF16),
        "gs": pltpu.VMEM((z.piece, 2 * mc), F32),
        "gat": pltpu.VMEM((z.n_space, z.piece, 2 * mc), F32),
    }
    sem = pltpu.SemaphoreType.DMA
    return {
        "sp": pltpu.VMEM((z.snaps, z.unknowns), BF16),
        "sa": pltpu.VMEM((z.snaps, z.unknowns), BF16),
        "cp": pltpu.VMEM((z.snaps, z.modes), BF16),
        "ca": pltpu.VMEM((z.snaps, z.modes), BF16),
        "op": pltpu.VMEM((z.rows, z.slots, bs, bs), BF16),
        "adj": pltpu.VMEM((z.modes, z.unknowns), BF16),
        "cpt": pltpu.VMEM((z.modes, z.snaps), BF16),
        "load": sem((5,)),
        "q_s": sem((z.chunks, z.n_snap - 1)),
        "q_r": sem((z.chunks, z.n_snap - 1)),
        "g_s": sem((z.chunks, z.lists)),
        "g_r": sem((z.chunks, z.lists)),
        "rs_s": sem((z.chunks,)),
        "rs_r": sem((z.chunks,)),
        "ag_s": sem((z.chunks,)),
        "ag_r": sem((z.chunks,)),
        "chunk": [dict(one) for _ in range(z.chunks)],
    }


def transposed(value):
    return value.astype(F32).T.astype(BF16)


def contract_last(a, b):
    return lax.dot_general(a, b, (((1,), (1,)), ((), ())), preferred_element_type=F32)


def loop(count, body):
    def step(i, carry):
        body(i)
        return carry

    lax.fori_loop(0, count, step, 0)


def kernel(z, sp_hbm, sa_hbm, cp_hbm, ca_hbm, op_hbm, counts, cols, ghosts,
           primal_out, applied_out, reduced_out, gram_out, s):
    space, snap = lax.axis_index("space"), lax.axis_index("snap")
    me = space * z.n_snap + snap
    bs, mc = z.bs, z.mc
    width = TILE_BLOCKS * bs

    loads = [
        pltpu.make_async_copy(source, s[name], s["load"].at[i])
        for i, (source, name) in enumerate(
            [(cp_hbm, "cp"), (sp_hbm, "sp"), (ca_hbm, "ca"), (sa_hbm, "sa"), (op_hbm, "op")]
        )
    ]
    for copy in loads:
        copy.start()

    barrier = pltpu.get_barrier_semaphore()

    def greet(i):
        other = lax.rem(me + 1 + i, z.devices)
        pl.semaphore_signal(
            barrier,
            inc=1,
            device_id=(lax.div(other, z.n_snap), lax.rem(other, z.n_snap)),
            device_id_type=MESH,
        )

    loop(z.devices - 1, greet)

    def columns(t):
        return pl.ds(pl.multiple_of(t * width, width), width)

    def project(c):
        coef = s["cpt"][c * mc:(c + 1) * mc, :]
        q = s["chunk"][c]["q"]

        def tile(t):
            part = jnp.dot(coef, s["sp"][:, columns(t)], preferred_element_type=F32).astype(BF16)
            for i in range(TILE_BLOCKS):
                q[t * TILE_BLOCKS + i] = part[:, i * bs:(i + 1) * bs]

        loop(z.tiles, tile)

    def partial_copy(c, i):
        k = s["chunk"][c]
        return pltpu.make_async_remote_copy(
            src_ref=k["q"],
            dst_ref=k["qr"].at[i],
            send_sem=s["q_s"].at[c, i],
            recv_sem=s["q_r"].at[c, i],
            device_id=(space, lax.rem(snap + 1 + i, z.n_snap)),
            device_id_type=MESH,
        )

    def ghost_copy(c, d):
        k = s["chunk"][c]
        first = z.rows + d * z.list_len
        return pltpu.make_async_remote_copy(
            src_ref=k["snd"].at[d],
            dst_ref=k["ext"].at[pl.ds(first, z.list_len)],
            send_sem=s["g_s"].at[c, d],
            recv_sem=s["g_r"].at[c, d],
            device_id=(space - OFFSETS[d], snap),
            device_id_type=MESH,
        )

    def inside(position):
        return (position >= 0) & (position < z.n_space)

    def own_modes(c):
        k = s["chunk"][c]
        for i in range(z.n_snap - 1):
            partial_copy(c, i).wait_recv()

        def block(b):
            total = k["q"][b].astype(F32)
            for i in range(z.n_snap - 1):
                total = total + k["qr"][i, b].astype(F32)
            total = total.astype(BF16)
            k["own"][b] = total
            k["ext"][b] = total
            k["st"][b, mc:, :] = total

        loop(z.rows, block)
        for d in range(z.lists):
            for t in range(z.list_len):
                k["snd"][d, t] = k["own"][ghosts[0, d, t]]

            @pl.when(inside(space - OFFSETS[d]))
            def _():
                ghost_copy(c, d).start()

            @pl.when(jnp.logical_not(inside(space + OFFSETS[d])))
            def _():
                first = z.rows + d * z.list_len
                k["ext"][first:first + z.list_len] = jnp.zeros((z.list_len, mc, bs), BF16)

    def keep(c, out, first):
        k = s["chunk"][c]
        for x, at, start, count in z.groups(c):
            @pl.when(snap == x)
            def _():
                def block(b):
                    out[at:at + count, pl.ds(pl.multiple_of(b * bs, bs), bs)] = k["st"][b, first + start:first + start + count, :]

                loop(z.rows, block)

    def apply(c):
        k = s["chunk"][c]
        for d in range(z.lists):
            @pl.when(inside(space + OFFSETS[d]))
            def _():
                ghost_copy(c, d).wait_recv()

        def row(b):
            live = counts[b]
            picked, mats = [], []
            for i in range(z.slots):
                value = k["ext"][cols[b, i]]
                picked.append(jnp.where(i < live, value, jnp.zeros_like(value)))
                mats.append(s["op"][b, i])
            result = contract_last(jnp.concatenate(picked, axis=1), jnp.concatenate(mats, axis=1))
            k["st"][b, :mc, :] = result.astype(BF16)

        loop(z.rows, row)

        def tile(t, total):
            right = jnp.concatenate([k["st"][t * TILE_BLOCKS + i] for i in range(TILE_BLOCKS)], axis=1)
            return total + contract_last(s["adj"][:, columns(t)], right)

        terms = lax.fori_loop(0, z.tiles, tile, jnp.zeros((z.modes, 2 * mc), F32))
        k["d"][...] = terms.astype(BF16).reshape(z.owners, z.piece, 2 * mc)
        for x, _, _, _ in z.groups(c):
            def send(o):
                same = (space == o) & (snap == x)

                @pl.when(same)
                def _():
                    k["rs"][me] = k["d"][o]

                @pl.when(jnp.logical_not(same))
                def _():
                    pltpu.make_async_remote_copy(
                        src_ref=k["d"].at[o],
                        dst_ref=k["rs"].at[me],
                        send_sem=s["rs_s"].at[c],
                        recv_sem=s["rs_r"].at[c],
                        device_id=(o, x),
                        device_id_type=MESH,
                    ).start()

            loop(z.owners, send)

    def settle(ref, count, sem):
        part = ref.at[pl.ds(0, count)]
        pltpu.make_async_copy(part, part, sem).wait()

    def among(c):
        found = snap == z.groups(c)[0][0]
        for x, _, _, _ in z.groups(c)[1:]:
            found = found | (snap == x)
        return found

    def add_up(c):
        k = s["chunk"][c]

        @pl.when(among(c) & (space < z.owners))
        def _():
            settle(k["rs"], z.devices - 1, s["rs_r"].at[c])
            total = lax.fori_loop(
                0,
                z.devices // 16,
                lambda i, t: t + jnp.sum(k["rs"][pl.ds(i * 16, 16)].astype(F32), axis=0),
                jnp.zeros((z.piece, 2 * mc), F32),
            )
            total = total * z.factor
            k["gs"][...] = total
            k["gat"][space] = total

            def send(i):
                pltpu.make_async_remote_copy(
                    src_ref=k["gs"],
                    dst_ref=k["gat"].at[space],
                    send_sem=s["ag_s"].at[c],
                    recv_sem=s["ag_r"].at[c],
                    device_id=(lax.rem(space + 1 + i, z.n_space), snap),
                    device_id_type=MESH,
                ).start()

            loop(z.n_space - 1, send)

    def finish(c):
        k = s["chunk"][c]
        for x, at, start, count in z.groups(c):
            @pl.when(snap == x)
            def _():
                @pl.when(space < z.owners)
                def _():
                    settle(k["gat"], z.owners - 1, s["ag_r"].at[c])

                if z.owners < z.n_space:
                    @pl.when(space >= z.owners)
                    def _():
                        settle(k["gat"], z.owners, s["ag_r"].at[c])

                whole = k["gat"][:z.owners].reshape(z.modes, 2 * mc)
                reduced_out[:, at:at + count] = whole[:, start:start + count]
                gram_out[:, at:at + count] = whole[:, mc + start:mc + start + count]

    loads[0].wait()
    s["cpt"][...] = transposed(s["cp"][...])
    loads[1].wait()
    project(0)
    pl.semaphore_wait(barrier, z.devices - 1)
    for c in range(z.chunks):
        if c:
            project(c)
        for i in range(z.n_snap - 1):
            partial_copy(c, i).start()

    loads[2].wait()
    cat = transposed(s["ca"][...])
    loads[3].wait()

    def adjoint(t):
        s["adj"][:, columns(t)] = jnp.dot(cat, s["sa"][:, columns(t)], preferred_element_type=F32).astype(BF16)

    loop(z.tiles, adjoint)
    loads[4].wait()

    last = z.chunks - 1
    for c in range(z.chunks):
        own_modes(c)
        keep(c, primal_out, mc)
        if c >= 1:
            apply(c - 1)
            keep(c - 1, applied_out, 0)
        if c >= 2:
            add_up(c - 2)
    if last >= 1:
        add_up(last - 1)
    apply(last)
    keep(last, applied_out, 0)
    add_up(last)
    for c in range(z.chunks):
        finish(c)

    for c in range(z.chunks):
        k = s["chunk"][c]
        for i in range(z.n_snap - 1):
            partial_copy(c, i).wait_send()
        for d in range(z.lists):
            @pl.when(inside(space - OFFSETS[d]))
            def _():
                ghost_copy(c, d).wait_send()

        count = len(z.groups(c)) * z.owners
        owner = among(c) & (space < z.owners)

        @pl.when(owner)
        def _():
            settle(k["rs"], count - 1, s["rs_s"].at[c])
            settle(k["gat"], z.n_space - 1, s["ag_s"].at[c])

        @pl.when(jnp.logical_not(owner))
        def _():
            settle(k["rs"], count, s["rs_s"].at[c])


def per_device(
    snaps_primal, snaps_adjoint, coef_primal, coef_adjoint, op_blocks, counts, col_index, ghost_send
):
    z = Sizes(
        lax.axis_size("space"), lax.axis_size("snap"), snaps_primal, coef_primal, op_blocks, ghost_send
    )
    any_spec = pl.BlockSpec(memory_space=pl.ANY)
    smem = pl.BlockSpec(memory_space=pltpu.SMEM)
    vmem = pl.BlockSpec(memory_space=pltpu.VMEM)
    names = scratch_of(z)
    flat, tree = jax.tree.flatten(names)

    def body(*refs):
        s = jax.tree.unflatten(tree, refs[12:])
        kernel(z, *refs[:12], s)

    flops = 2 * z.unknowns * z.modes * (2 * z.snaps + z.slots * z.bs + 2 * z.modes)
    return pl.pallas_call(
        body,
        out_shape=(
            jax.ShapeDtypeStruct((z.share, z.unknowns), BF16),
            jax.ShapeDtypeStruct((z.share, z.unknowns), BF16),
            jax.ShapeDtypeStruct((z.modes, z.share), F32),
            jax.ShapeDtypeStruct((z.modes, z.share), F32),
        ),
        in_specs=[any_spec] * 5 + [smem] * 3,
        out_specs=[vmem] * 4,
        scratch_shapes=flat,
        cost_estimate=pl.CostEstimate(flops=flops, bytes_accessed=10_000_000, transcendentals=0),
        compiler_params=pltpu.CompilerParams(
            collective_id=0, has_side_effects=True, vmem_limit_bytes=58 * 1024 * 1024
        ),
    )(snaps_primal, snaps_adjoint, coef_primal, coef_adjoint, op_blocks, counts, col_index, ghost_send)


def solution(mesh):
    placed = (
        P("snap", "space"),
        P("snap", "space"),
        P("snap", None),
        P("snap", None),
        P("space", None, None, None),
        P("space"),
        P("space", None),
        P("space", None, None),
    )
    return jax.shard_map(
        per_device,
        mesh=mesh,
        in_specs=placed,
        out_specs=(P("snap", "space"), P("snap", "space"), P(None, "snap"), P(None, "snap")),
        check_vma=False,
    )
```

```python
import math

import jax
import jax.numpy as jnp
from jax import lax
from jax.experimental import pallas as pl
from jax.experimental.pallas import tpu as pltpu
from jax.sharding import PartitionSpec as P

MESH = pl.DeviceIdType.MESH
BF16 = jnp.bfloat16
F32 = jnp.float32
OFFSETS = (-2, -1, 1, 2)
TILE_BLOCKS = 4
CHUNK = 64


class Sizes:
    def __init__(self, n_space, n_snap, snaps, coef, op_blocks, ghost_send):
        self.n_space, self.n_snap = n_space, n_snap
        self.devices = n_space * n_snap
        self.snaps, self.unknowns = snaps.shape
        self.modes = coef.shape[1]
        self.share = self.modes // n_snap
        self.rows, self.slots, self.bs = op_blocks.shape[:3]
        self.lists, self.list_len = ghost_send.shape[1:]
        self.mc = CHUNK
        self.chunks = self.modes // self.mc
        self.piece = max(16, self.modes // n_space)
        self.owners = self.modes // self.piece
        self.tiles = self.rows // TILE_BLOCKS
        self.factor = 1.0 / math.sqrt(self.unknowns * n_space)

    def groups(self, c):
        first, last = c * self.mc, (c + 1) * self.mc
        found = []
        for x in range(self.n_snap):
            lo, hi = max(first, x * self.share), min(last, (x + 1) * self.share)
            if lo < hi:
                found.append((x, lo - x * self.share, lo - first, hi - lo))
        return found


def scratch_of(z):
    b, mc, bs = z.rows, z.mc, z.bs
    one = {
        "q": pltpu.VMEM((b, mc, bs), BF16),
        "qr": pltpu.VMEM((z.n_snap - 1, b, mc, bs), BF16),
        "own": pltpu.VMEM((b, mc, bs), BF16),
        "ext": pltpu.VMEM((b + z.lists * z.list_len, mc, bs), BF16),
        "snd": pltpu.VMEM((z.lists, z.list_len, mc, bs), BF16),
        "d": pltpu.VMEM((z.owners, z.piece, 2 * mc), BF16),
        "rs": pltpu.VMEM((z.devices, z.piece, 2 * mc), BF16),
        "gs": pltpu.VMEM((z.piece, 2 * mc), F32),
        "gat": pltpu.VMEM((z.n_space, z.piece, 2 * mc), F32),
    }
    sem = pltpu.SemaphoreType.DMA
    return {
        "sp": pltpu.VMEM((z.snaps, z.unknowns), BF16),
        "sa": pltpu.VMEM((z.snaps, z.unknowns), BF16),
        "cp": pltpu.VMEM((z.snaps, z.modes), BF16),
        "ca": pltpu.VMEM((z.snaps, z.modes), BF16),
        "op": pltpu.VMEM((z.rows, z.slots, bs, bs), BF16),
        "adj": pltpu.VMEM((z.modes, z.unknowns), BF16),
        "v": pltpu.VMEM((z.tiles, z.modes, TILE_BLOCKS * z.slots * bs), BF16),
        "po": pltpu.VMEM((z.share, z.unknowns), BF16),
        "ao": pltpu.VMEM((z.share, z.unknowns), BF16),
        "ro": pltpu.VMEM((z.modes, z.share), F32),
        "go": pltpu.VMEM((z.modes, z.share), F32),
        "store": sem((4,)),
        "cpt": pltpu.VMEM((z.modes, z.snaps), BF16),
        "load": sem((5,)),
        "q_s": sem((z.chunks, z.n_snap - 1)),
        "q_r": sem((z.chunks, z.n_snap - 1)),
        "g_s": sem((z.chunks, z.lists)),
        "g_r": sem((z.chunks, z.lists)),
        "rs_s": sem((z.chunks,)),
        "rs_r": sem((z.chunks,)),
        "ag_s": sem((z.chunks,)),
        "ag_r": sem((z.chunks,)),
        "chunk": [dict(one) for _ in range(z.chunks)],
    }


def transposed(value):
    return value.astype(F32).T.astype(BF16)


def contract_last(a, b):
    return lax.dot_general(a, b, (((1,), (1,)), ((), ())), preferred_element_type=F32)


def loop(count, body):
    def step(i, carry):
        body(i)
        return carry

    lax.fori_loop(0, count, step, 0)


def kernel(z, sp_hbm, sa_hbm, cp_hbm, ca_hbm, op_hbm, counts, cols, ghosts,
           primal_out, applied_out, reduced_out, gram_out, s):
    space, snap = lax.axis_index("space"), lax.axis_index("snap")
    me = space * z.n_snap + snap
    bs, mc = z.bs, z.mc
    width = TILE_BLOCKS * bs

    loads = [
        pltpu.make_async_copy(source, s[name], s["load"].at[i])
        for i, (source, name) in enumerate(
            [(cp_hbm, "cp"), (sp_hbm, "sp"), (ca_hbm, "ca"), (sa_hbm, "sa"), (op_hbm, "op")]
        )
    ]
    for copy in loads:
        copy.start()

    barrier = pltpu.get_barrier_semaphore()

    def greet(i):
        other = lax.rem(me + 1 + i, z.devices)
        pl.semaphore_signal(
            barrier,
            inc=1,
            device_id=(lax.div(other, z.n_snap), lax.rem(other, z.n_snap)),
            device_id_type=MESH,
        )

    loop(z.devices - 1, greet)

    def columns(t):
        return pl.ds(pl.multiple_of(t * width, width), width)

    def project(c):
        coef = s["cpt"][c * mc:(c + 1) * mc, :]
        q = s["chunk"][c]["q"]

        def tile(t):
            part = jnp.dot(coef, s["sp"][:, columns(t)], preferred_element_type=F32).astype(BF16)
            for i in range(TILE_BLOCKS):
                q[t * TILE_BLOCKS + i] = part[:, i * bs:(i + 1) * bs]

        loop(z.tiles, tile)

    def partial_copy(c, i):
        k = s["chunk"][c]
        return pltpu.make_async_remote_copy(
            src_ref=k["q"],
            dst_ref=k["qr"].at[i],
            send_sem=s["q_s"].at[c, i],
            recv_sem=s["q_r"].at[c, i],
            device_id=(space, lax.rem(snap + 1 + i, z.n_snap)),
            device_id_type=MESH,
        )

    def ghost_copy(c, d):
        k = s["chunk"][c]
        first = z.rows + d * z.list_len
        return pltpu.make_async_remote_copy(
            src_ref=k["snd"].at[d],
            dst_ref=k["ext"].at[pl.ds(first, z.list_len)],
            send_sem=s["g_s"].at[c, d],
            recv_sem=s["g_r"].at[c, d],
            device_id=(space - OFFSETS[d], snap),
            device_id_type=MESH,
        )

    def inside(position):
        return (position >= 0) & (position < z.n_space)

    def blocks_of(t):
        return [t * TILE_BLOCKS + i for i in range(TILE_BLOCKS)]

    def carry_operator(t):
        for i, b in enumerate(blocks_of(t)):
            live = counts[b]
            rows = s["adj"][:, pl.ds(pl.multiple_of(b * bs, bs), bs)]
            mats = jnp.concatenate([s["op"][b, j] for j in range(z.slots)], axis=1)
            part = jnp.dot(rows, mats, preferred_element_type=F32)
            for j in range(z.slots):
                value = part[:, j * bs:(j + 1) * bs]
                value = jnp.where(j < live, value, jnp.zeros_like(value)).astype(BF16)
                first = (i * z.slots + j) * bs
                s["v"][t, :, first:first + bs] = value

    def own_modes(c):
        k = s["chunk"][c]
        for i in range(z.n_snap - 1):
            partial_copy(c, i).wait_recv()

        def tile(t):
            for b in blocks_of(t):
                total = k["q"][b].astype(F32)
                for i in range(z.n_snap - 1):
                    total = total + k["qr"][i, b].astype(F32)
                total = total.astype(BF16)
                k["own"][b] = total
                k["ext"][b] = total

        loop(z.tiles, tile)
        for d in range(z.lists):
            for t in range(z.list_len):
                k["snd"][d, t] = k["own"][ghosts[0, d, t]]

            @pl.when(inside(space - OFFSETS[d]))
            def _():
                ghost_copy(c, d).start()

            @pl.when(jnp.logical_not(inside(space + OFFSETS[d])))
            def _():
                first = z.rows + d * z.list_len
                k["ext"][first:first + z.list_len] = jnp.zeros((z.list_len, mc, bs), BF16)

        def gram(t, total):
            right = jnp.concatenate([k["own"][b] for b in blocks_of(t)], axis=1)
            return total + contract_last(s["adj"][:, columns(t)], right)

        terms = lax.fori_loop(0, z.tiles, gram, jnp.zeros((z.modes, mc), F32))
        k["d"][:, :, mc:] = terms.astype(BF16).reshape(z.owners, z.piece, mc)

        for x, at, start, count in z.groups(c):
            @pl.when(snap == x)
            def _():
                def keep(t):
                    for b in blocks_of(t):
                        s["po"][at:at + count, pl.ds(pl.multiple_of(b * bs, bs), bs)] = k["own"][b, start:start + count, :]

                loop(z.tiles, keep)

    def terms_of(c):
        k = s["chunk"][c]
        for d in range(z.lists):
            @pl.when(inside(space + OFFSETS[d]))
            def _():
                ghost_copy(c, d).wait_recv()

        def tile(t, total):
            picked = [k["ext"][cols[j, b]] for b in blocks_of(t) for j in range(z.slots)]
            return total + contract_last(s["v"][t], jnp.concatenate(picked, axis=1))

        terms = lax.fori_loop(0, z.tiles, tile, jnp.zeros((z.modes, mc), F32))
        k["d"][:, :, :mc] = terms.astype(BF16).reshape(z.owners, z.piece, mc)
        for x, _, _, _ in z.groups(c):
            def send(i):
                o = lax.rem(space + 1 + i, z.owners)
                same = (space == o) & (snap == x)

                @pl.when(same)
                def _():
                    k["rs"][me] = k["d"][o]

                @pl.when(jnp.logical_not(same))
                def _():
                    pltpu.make_async_remote_copy(
                        src_ref=k["d"].at[o],
                        dst_ref=k["rs"].at[me],
                        send_sem=s["rs_s"].at[c],
                        recv_sem=s["rs_r"].at[c],
                        device_id=(o, x),
                        device_id_type=MESH,
                    ).start()

            loop(z.owners, send)

    def apply(c, low, high):
        k = s["chunk"][c]
        for x, at, start, count in z.groups(c):
            @pl.when(snap == x)
            def _():
                def tile(t):
                    for b in blocks_of(low + t):
                        live = counts[b]
                        picked, mats = [], []
                        for j in range(z.slots):
                            value = k["ext"][cols[j, b]][start:start + count]
                            picked.append(jnp.where(j < live, value, jnp.zeros_like(value)))
                            mats.append(s["op"][b, j])
                        result = contract_last(jnp.concatenate(picked, axis=1), jnp.concatenate(mats, axis=1))
                        s["ao"][at:at + count, pl.ds(pl.multiple_of(b * bs, bs), bs)] = result.astype(BF16)

                loop(high - low, tile)

    def settle(ref, count, sem):
        part = ref.at[pl.ds(0, count)]
        pltpu.make_async_copy(part, part, sem).wait()

    def among(c):
        found = snap == z.groups(c)[0][0]
        for x, _, _, _ in z.groups(c)[1:]:
            found = found | (snap == x)
        return found

    def add_up(c):
        k = s["chunk"][c]

        @pl.when(among(c) & (space < z.owners))
        def _():
            settle(k["rs"], z.devices - 1, s["rs_r"].at[c])
            total = lax.fori_loop(
                0,
                z.devices // 16,
                lambda i, t: t + jnp.sum(k["rs"][pl.ds(i * 16, 16)].astype(F32), axis=0),
                jnp.zeros((z.piece, 2 * mc), F32),
            )
            total = total * z.factor
            k["gs"][...] = total
            k["gat"][space] = total

            def send(i):
                pltpu.make_async_remote_copy(
                    src_ref=k["gs"],
                    dst_ref=k["gat"].at[space],
                    send_sem=s["ag_s"].at[c],
                    recv_sem=s["ag_r"].at[c],
                    device_id=(lax.rem(space + 1 + i, z.n_space), snap),
                    device_id_type=MESH,
                ).start()

            loop(z.n_space - 1, send)

    def finish(c):
        k = s["chunk"][c]
        for x, at, start, count in z.groups(c):
            @pl.when(snap == x)
            def _():
                @pl.when(space < z.owners)
                def _():
                    settle(k["gat"], z.owners - 1, s["ag_r"].at[c])

                if z.owners < z.n_space:
                    @pl.when(space >= z.owners)
                    def _():
                        settle(k["gat"], z.owners, s["ag_r"].at[c])

                whole = k["gat"][:z.owners].reshape(z.modes, 2 * mc)
                s["ro"][:, at:at + count] = whole[:, start:start + count]
                s["go"][:, at:at + count] = whole[:, mc + start:mc + start + count]

    loads[0].wait()
    s["cpt"][...] = transposed(s["cp"][...])
    loads[1].wait()
    project(0)
    pl.semaphore_wait(barrier, z.devices - 1)
    for c in range(z.chunks):
        if c:
            project(c)
        for i in range(z.n_snap - 1):
            partial_copy(c, i).start()

    loads[2].wait()
    cat = transposed(s["ca"][...])
    loads[3].wait()

    def adjoint(t):
        s["adj"][:, columns(t)] = jnp.dot(cat, s["sa"][:, columns(t)], preferred_element_type=F32).astype(BF16)

    loop(z.tiles, adjoint)
    loads[4].wait()
    loop(z.tiles, carry_operator)

    stores = [
        pltpu.make_async_copy(s[name], target, s["store"].at[i])
        for i, (name, target) in enumerate(
            [("po", primal_out), ("ao", applied_out), ("ro", reduced_out), ("go", gram_out)]
        )
    ]
    last = z.chunks - 1
    half = z.tiles // 2
    for c in range(z.chunks):
        own_modes(c)
        if c == last:
            stores[0].start()
        if c >= 1:
            terms_of(c - 1)
            apply(c - 1, 0, z.tiles)
        if c >= 2:
            add_up(c - 2)
    terms_of(last)
    if last:
        add_up(last - 1)
    apply(last, 0, half)
    add_up(last)
    apply(last, half, z.tiles)
    stores[1].start()
    for c in range(z.chunks):
        finish(c)
    stores[2].start()
    stores[3].start()

    for c in range(z.chunks):
        k = s["chunk"][c]
        for i in range(z.n_snap - 1):
            partial_copy(c, i).wait_send()
        for d in range(z.lists):
            @pl.when(inside(space - OFFSETS[d]))
            def _():
                ghost_copy(c, d).wait_send()

        count = len(z.groups(c)) * z.owners
        owner = among(c) & (space < z.owners)

        @pl.when(owner)
        def _():
            settle(k["rs"], count - 1, s["rs_s"].at[c])
            settle(k["gat"], z.n_space - 1, s["ag_s"].at[c])

        @pl.when(jnp.logical_not(owner))
        def _():
            settle(k["rs"], count, s["rs_s"].at[c])

    for copy in stores:
        copy.wait()


def hand_over(*refs):
    copies = [pltpu.make_async_copy(refs[i], refs[4 + i], refs[8].at[i]) for i in range(4)]
    for copy in copies:
        copy.start()
    for copy in copies:
        copy.wait()


def per_device(
    snaps_primal, snaps_adjoint, coef_primal, coef_adjoint, op_blocks, counts, col_index, ghost_send
):
    z = Sizes(
        lax.axis_size("space"), lax.axis_size("snap"), snaps_primal, coef_primal, op_blocks, ghost_send
    )
    any_spec = pl.BlockSpec(memory_space=pl.ANY)
    smem = pl.BlockSpec(memory_space=pltpu.SMEM)
    names = scratch_of(z)
    flat, tree = jax.tree.flatten(names)

    def body(*refs):
        s = jax.tree.unflatten(tree, refs[12:])
        kernel(z, *refs[:12], s)

    flops = 2 * z.unknowns * z.modes * (2 * z.snaps + z.slots * z.bs + 2 * z.modes)
    shapes = (
        jax.ShapeDtypeStruct((z.share, z.unknowns), BF16),
        jax.ShapeDtypeStruct((z.share, z.unknowns), BF16),
        jax.ShapeDtypeStruct((z.modes, z.share), F32),
        jax.ShapeDtypeStruct((z.modes, z.share), F32),
    )
    results = pl.pallas_call(
        body,
        out_shape=shapes,
        in_specs=[any_spec] * 5 + [smem] * 3,
        out_specs=[any_spec] * 4,
        scratch_shapes=flat,
        cost_estimate=pl.CostEstimate(flops=flops, bytes_accessed=10_000_000, transcendentals=0),
        compiler_params=pltpu.CompilerParams(
            collective_id=0, has_side_effects=True, vmem_limit_bytes=58 * 1024 * 1024
        ),
    )(snaps_primal, snaps_adjoint, coef_primal, coef_adjoint, op_blocks, counts, col_index.T, ghost_send)
    return pl.pallas_call(
        hand_over,
        out_shape=shapes,
        in_specs=[any_spec] * 4,
        out_specs=[any_spec] * 4,
        scratch_shapes=[pltpu.SemaphoreType.DMA((4,))],
    )(*results)


def solution(mesh):
    placed = (
        P("snap", "space"),
        P("snap", "space"),
        P("snap", None),
        P("snap", None),
        P("space", None, None, None),
        P("space"),
        P("space", None),
        P("space", None, None),
    )
    return jax.shard_map(
        per_device,
        mesh=mesh,
        in_specs=placed,
        out_specs=(P("snap", "space"), P("snap", "space"), P(None, "snap"), P(None, "snap")),
        check_vma=False,
    )
```

```python
import math

import jax
import jax.numpy as jnp
from jax import lax
from jax.experimental import pallas as pl
from jax.experimental.pallas import tpu as pltpu
from jax.sharding import PartitionSpec as P

MESH = pl.DeviceIdType.MESH
BF16 = jnp.bfloat16
F32 = jnp.float32
OFFSETS = (-2, -1, 1, 2)
TILE_BLOCKS = 4
CHUNKS = ((64,), (64,), (48, 48), (32,))


class Sizes:
    def __init__(self, n_space, n_snap, snaps, coef, op_blocks, ghost_send):
        self.n_space, self.n_snap = n_space, n_snap
        self.devices = n_space * n_snap
        self.snaps, self.unknowns = snaps.shape
        self.modes = coef.shape[1]
        self.share = self.modes // n_snap
        self.rows, self.slots, self.bs = op_blocks.shape[:3]
        self.lists, self.list_len = ghost_send.shape[1:]
        self.parts, self.sums, first = [], [], 0
        for g, sizes in enumerate(CHUNKS):
            self.sums.append((first, sum(sizes)))
            for size in sizes:
                self.parts.append((first, size, g))
                first += size
        assert first == self.modes
        self.chunks = len(self.parts)
        self.piece = max(16, self.modes // n_space)
        self.owners = self.modes // self.piece
        self.tiles = self.rows // TILE_BLOCKS
        self.factor = 1.0 / math.sqrt(self.unknowns * n_space)

    def groups(self, first, size):
        last = first + size
        found = []
        for x in range(self.n_snap):
            lo, hi = max(first, x * self.share), min(last, (x + 1) * self.share)
            if lo < hi:
                found.append((x, lo - x * self.share, lo - first, hi - lo))
        return found


def chunk_scratch(z, mc):
    b, bs = z.rows, z.bs
    return {
        "q": pltpu.VMEM((b, mc, bs), BF16),
        "qr": pltpu.VMEM((z.n_snap - 1, b, mc, bs), BF16),
        "own": pltpu.VMEM((b, mc, bs), BF16),
        "ext": pltpu.VMEM((b + z.lists * z.list_len, mc, bs), BF16),
        "snd": pltpu.VMEM((z.lists, z.list_len, mc, bs), BF16),
    }


def sum_scratch(z, mc):
    return {
        "d": pltpu.VMEM((z.owners, z.piece, 2 * mc), BF16),
        "rs": pltpu.VMEM((z.devices, z.piece, 2 * mc), BF16),
        "gs": pltpu.VMEM((z.piece, 2 * mc), F32),
        "gat": pltpu.VMEM((z.n_space, z.piece, 2 * mc), F32),
    }


def scratch_of(z):
    bs = z.bs
    sem = pltpu.SemaphoreType.DMA
    return {
        "sp": pltpu.VMEM((z.snaps, z.unknowns), BF16),
        "sa": pltpu.VMEM((z.snaps, z.unknowns), BF16),
        "cp": pltpu.VMEM((z.snaps, z.modes), BF16),
        "ca": pltpu.VMEM((z.snaps, z.modes), BF16),
        "op": pltpu.VMEM((z.rows, z.slots, bs, bs), BF16),
        "adj": pltpu.VMEM((z.modes, z.unknowns), BF16),
        "v": pltpu.VMEM((z.tiles, z.modes, TILE_BLOCKS * z.slots * bs), BF16),
        "po": pltpu.VMEM((z.share, z.unknowns), BF16),
        "ao": pltpu.VMEM((z.share, z.unknowns), BF16),
        "ro": pltpu.VMEM((z.modes, z.share), F32),
        "go": pltpu.VMEM((z.modes, z.share), F32),
        "store": sem((4,)),
        "cpt": pltpu.VMEM((z.modes, z.snaps), BF16),
        "load": sem((5,)),
        "q_s": sem((z.chunks, z.n_snap - 1)),
        "q_r": sem((z.chunks, z.n_snap - 1)),
        "g_s": sem((z.chunks, z.lists)),
        "g_r": sem((z.chunks, z.lists)),
        "rs_s": sem((len(z.sums),)),
        "rs_r": sem((len(z.sums),)),
        "ag_s": sem((len(z.sums),)),
        "ag_r": sem((len(z.sums),)),
        "chunk": [chunk_scratch(z, size) for _, size, _ in z.parts],
        "sum": [sum_scratch(z, size) for _, size in z.sums],
    }


def transposed(value):
    return value.astype(F32).T.astype(BF16)


def contract_last(a, b):
    return lax.dot_general(a, b, (((1,), (1,)), ((), ())), preferred_element_type=F32)


def loop(count, body):
    def step(i, carry):
        body(i)
        return carry

    lax.fori_loop(0, count, step, 0)


def kernel(z, sp_hbm, sa_hbm, cp_hbm, ca_hbm, op_hbm, counts, cols, ghosts,
           primal_out, applied_out, reduced_out, gram_out, s):
    space, snap = lax.axis_index("space"), lax.axis_index("snap")
    me = space * z.n_snap + snap
    bs = z.bs
    width = TILE_BLOCKS * bs

    loads = [
        pltpu.make_async_copy(source, s[name], s["load"].at[i])
        for i, (source, name) in enumerate(
            [(cp_hbm, "cp"), (sp_hbm, "sp"), (ca_hbm, "ca"), (sa_hbm, "sa"), (op_hbm, "op")]
        )
    ]
    for copy in loads[:2]:
        copy.start()

    barrier = pltpu.get_barrier_semaphore()

    def greet(i):
        other = lax.rem(me + 1 + i, z.devices)
        pl.semaphore_signal(
            barrier,
            inc=1,
            device_id=(lax.div(other, z.n_snap), lax.rem(other, z.n_snap)),
            device_id_type=MESH,
        )

    loop(z.devices - 1, greet)

    def columns(t):
        return pl.ds(pl.multiple_of(t * width, width), width)

    def project(c):
        first, mc, _ = z.parts[c]
        coef = s["cpt"][first:first + mc, :]
        q = s["chunk"][c]["q"]

        def tile(t):
            part = jnp.dot(coef, s["sp"][:, columns(t)], preferred_element_type=F32).astype(BF16)
            for i in range(TILE_BLOCKS):
                q[t * TILE_BLOCKS + i] = part[:, i * bs:(i + 1) * bs]

        loop(z.tiles, tile)

    def partial_copy(c, i):
        k = s["chunk"][c]
        return pltpu.make_async_remote_copy(
            src_ref=k["q"],
            dst_ref=k["qr"].at[i],
            send_sem=s["q_s"].at[c, i],
            recv_sem=s["q_r"].at[c, i],
            device_id=(space, lax.rem(snap + 1 + i, z.n_snap)),
            device_id_type=MESH,
        )

    def ghost_copy(c, d):
        k = s["chunk"][c]
        first = z.rows + d * z.list_len
        return pltpu.make_async_remote_copy(
            src_ref=k["snd"].at[d],
            dst_ref=k["ext"].at[pl.ds(first, z.list_len)],
            send_sem=s["g_s"].at[c, d],
            recv_sem=s["g_r"].at[c, d],
            device_id=(space - OFFSETS[d], snap),
            device_id_type=MESH,
        )

    def inside(position):
        return (position >= 0) & (position < z.n_space)

    def blocks_of(t):
        return [t * TILE_BLOCKS + i for i in range(TILE_BLOCKS)]

    def carry_operator(t):
        for i, b in enumerate(blocks_of(t)):
            live = counts[b]
            rows = s["adj"][:, pl.ds(pl.multiple_of(b * bs, bs), bs)]
            mats = jnp.concatenate([s["op"][b, j] for j in range(z.slots)], axis=1)
            part = jnp.dot(rows, mats, preferred_element_type=F32)
            for j in range(z.slots):
                value = part[:, j * bs:(j + 1) * bs]
                value = jnp.where(j < live, value, jnp.zeros_like(value)).astype(BF16)
                first = (i * z.slots + j) * bs
                s["v"][t, :, first:first + bs] = value

    def own_modes(c):
        k = s["chunk"][c]
        first_mode, mc, g = z.parts[c]
        sum_first, sum_size = z.sums[g]
        shift = first_mode - sum_first
        for i in range(z.n_snap - 1):
            partial_copy(c, i).wait_recv()

        def tile(t):
            for b in blocks_of(t):
                total = k["q"][b].astype(F32)
                for i in range(z.n_snap - 1):
                    total = total + k["qr"][i, b].astype(F32)
                total = total.astype(BF16)
                k["own"][b] = total
                k["ext"][b] = total

        loop(z.tiles, tile)
        for d in range(z.lists):
            for t in range(z.list_len):
                k["snd"][d, t] = k["own"][ghosts[0, d, t]]

            @pl.when(inside(space - OFFSETS[d]))
            def _():
                ghost_copy(c, d).start()

            @pl.when(jnp.logical_not(inside(space + OFFSETS[d])))
            def _():
                first = z.rows + d * z.list_len
                k["ext"][first:first + z.list_len] = jnp.zeros((z.list_len, mc, bs), BF16)

        def gram(t, total):
            right = jnp.concatenate([k["own"][b] for b in blocks_of(t)], axis=1)
            return total + contract_last(s["adj"][:, columns(t)], right)

        terms = lax.fori_loop(0, z.tiles, gram, jnp.zeros((z.modes, mc), F32))
        lane = sum_size + shift
        s["sum"][g]["d"][:, :, lane:lane + mc] = terms.astype(BF16).reshape(z.owners, z.piece, mc)

        for x, at, start, count in z.groups(first_mode, mc):
            @pl.when(snap == x)
            def _():
                def keep(t):
                    for b in blocks_of(t):
                        s["po"][at:at + count, pl.ds(pl.multiple_of(b * bs, bs), bs)] = k["own"][b, start:start + count, :]

                loop(z.tiles, keep)

    def terms_of(c):
        k = s["chunk"][c]
        first_mode, mc, g = z.parts[c]
        shift = first_mode - z.sums[g][0]
        for d in range(z.lists):
            @pl.when(inside(space + OFFSETS[d]))
            def _():
                ghost_copy(c, d).wait_recv()

        def tile(t, total):
            picked = [k["ext"][cols[j, b]] for b in blocks_of(t) for j in range(z.slots)]
            return total + contract_last(s["v"][t], jnp.concatenate(picked, axis=1))

        terms = lax.fori_loop(0, z.tiles, tile, jnp.zeros((z.modes, mc), F32))
        s["sum"][g]["d"][:, :, shift:shift + mc] = terms.astype(BF16).reshape(z.owners, z.piece, mc)

    def share_out(g):
        k = s["sum"][g]
        for x, _, _, _ in z.groups(*z.sums[g]):
            def send(i):
                o = lax.rem(space + 1 + i, z.owners)
                same = (space == o) & (snap == x)

                @pl.when(same)
                def _():
                    k["rs"][me] = k["d"][o]

                @pl.when(jnp.logical_not(same))
                def _():
                    pltpu.make_async_remote_copy(
                        src_ref=k["d"].at[o],
                        dst_ref=k["rs"].at[me],
                        send_sem=s["rs_s"].at[g],
                        recv_sem=s["rs_r"].at[g],
                        device_id=(o, x),
                        device_id_type=MESH,
                    ).start()

            loop(z.owners, send)

    def apply(c, low, high):
        k = s["chunk"][c]
        for x, at, start, count in z.groups(*z.parts[c][:2]):
            @pl.when(snap == x)
            def _():
                def tile(t):
                    for b in blocks_of(low + t):
                        live = counts[b]
                        picked, mats = [], []
                        for j in range(z.slots):
                            value = k["ext"][cols[j, b]][start:start + count]
                            picked.append(jnp.where(j < live, value, jnp.zeros_like(value)))
                            mats.append(s["op"][b, j])
                        result = contract_last(jnp.concatenate(picked, axis=1), jnp.concatenate(mats, axis=1))
                        s["ao"][at:at + count, pl.ds(pl.multiple_of(b * bs, bs), bs)] = result.astype(BF16)

                loop(high - low, tile)

    def settle(ref, count, sem):
        part = ref.at[pl.ds(0, count)]
        pltpu.make_async_copy(part, part, sem).wait()

    def among(g):
        found = snap == z.groups(*z.sums[g])[0][0]
        for x, _, _, _ in z.groups(*z.sums[g])[1:]:
            found = found | (snap == x)
        return found

    def add_up(g):
        k = s["sum"][g]
        mc = z.sums[g][1]

        @pl.when(among(g) & (space < z.owners))
        def _():
            settle(k["rs"], z.devices - 1, s["rs_r"].at[g])
            total = lax.fori_loop(
                0,
                z.devices // 16,
                lambda i, t: t + jnp.sum(k["rs"][pl.ds(i * 16, 16)].astype(F32), axis=0),
                jnp.zeros((z.piece, 2 * mc), F32),
            )
            total = total * z.factor
            k["gs"][...] = total
            k["gat"][space] = total

            def send(i):
                pltpu.make_async_remote_copy(
                    src_ref=k["gs"],
                    dst_ref=k["gat"].at[space],
                    send_sem=s["ag_s"].at[g],
                    recv_sem=s["ag_r"].at[g],
                    device_id=(lax.rem(space + 1 + i, z.n_space), snap),
                    device_id_type=MESH,
                ).start()

            loop(z.n_space - 1, send)

    def finish(g):
        k = s["sum"][g]
        mc = z.sums[g][1]
        for x, at, start, count in z.groups(*z.sums[g]):
            @pl.when(snap == x)
            def _():
                @pl.when(space < z.owners)
                def _():
                    settle(k["gat"], z.owners - 1, s["ag_r"].at[g])

                if z.owners < z.n_space:
                    @pl.when(space >= z.owners)
                    def _():
                        settle(k["gat"], z.owners, s["ag_r"].at[g])

                whole = k["gat"][:z.owners].reshape(z.modes, 2 * mc)
                s["ro"][:, at:at + count] = whole[:, start:start + count]
                s["go"][:, at:at + count] = whole[:, mc + start:mc + start + count]

    loads[0].wait()
    s["cpt"][...] = transposed(s["cp"][...])
    loads[1].wait()
    for copy in loads[2:]:
        copy.start()
    project(0)
    pl.semaphore_wait(barrier, z.devices - 1)
    for c in range(z.chunks):
        if c:
            project(c)
        for i in range(z.n_snap - 1):
            partial_copy(c, i).start()

    loads[2].wait()
    cat = transposed(s["ca"][...])
    loads[3].wait()

    def adjoint(t):
        s["adj"][:, columns(t)] = jnp.dot(cat, s["sa"][:, columns(t)], preferred_element_type=F32).astype(BF16)

    loop(z.tiles, adjoint)
    loads[4].wait()
    loop(z.tiles, carry_operator)

    stores = [
        pltpu.make_async_copy(s[name], target, s["store"].at[i])
        for i, (name, target) in enumerate(
            [("po", primal_out), ("ao", applied_out), ("ro", reduced_out), ("go", gram_out)]
        )
    ]
    last = z.chunks - 1

    def ends(c):
        return c == last or z.parts[c + 1][2] != z.parts[c][2]

    def reduced_terms(c):
        terms_of(c)
        if ends(c):
            share_out(z.parts[c][2])

    pending = []
    for c in range(z.chunks):
        own_modes(c)
        if c == last:
            stores[0].start()
        if c:
            reduced_terms(c - 1)
            if c < last:
                apply(c - 1, 0, z.tiles)
                for g in pending:
                    add_up(g)
                pending = [z.parts[c - 1][2]] if ends(c - 1) else []
            elif ends(c - 1):
                pending.append(z.parts[c - 1][2])
    reduced_terms(last)
    for g in pending:
        add_up(g)
    apply(last - 1, 0, z.tiles)
    add_up(z.parts[last][2])
    apply(last, 0, z.tiles)
    stores[1].start()
    for g in range(len(z.sums)):
        finish(g)
    stores[2].start()
    stores[3].start()

    for c in range(z.chunks):
        for i in range(z.n_snap - 1):
            partial_copy(c, i).wait_send()
        for d in range(z.lists):
            @pl.when(inside(space - OFFSETS[d]))
            def _():
                ghost_copy(c, d).wait_send()

    for g in range(len(z.sums)):
        k = s["sum"][g]
        count = len(z.groups(*z.sums[g])) * z.owners
        owner = among(g) & (space < z.owners)

        @pl.when(owner)
        def _():
            settle(k["rs"], count - 1, s["rs_s"].at[g])
            settle(k["gat"], z.n_space - 1, s["ag_s"].at[g])

        @pl.when(jnp.logical_not(owner))
        def _():
            settle(k["rs"], count, s["rs_s"].at[g])

    for copy in stores:
        copy.wait()


def hand_over(*refs):
    copies = [pltpu.make_async_copy(refs[i], refs[4 + i], refs[8].at[i]) for i in range(4)]
    for copy in copies:
        copy.start()
    for copy in copies:
        copy.wait()


def per_device(
    snaps_primal, snaps_adjoint, coef_primal, coef_adjoint, op_blocks, counts, col_index, ghost_send
):
    z = Sizes(
        lax.axis_size("space"), lax.axis_size("snap"), snaps_primal, coef_primal, op_blocks, ghost_send
    )
    any_spec = pl.BlockSpec(memory_space=pl.ANY)
    smem = pl.BlockSpec(memory_space=pltpu.SMEM)
    names = scratch_of(z)
    flat, tree = jax.tree.flatten(names)

    def body(*refs):
        s = jax.tree.unflatten(tree, refs[12:])
        kernel(z, *refs[:12], s)

    flops = 2 * z.unknowns * z.modes * (2 * z.snaps + z.slots * z.bs + 2 * z.modes)
    shapes = (
        jax.ShapeDtypeStruct((z.share, z.unknowns), BF16),
        jax.ShapeDtypeStruct((z.share, z.unknowns), BF16),
        jax.ShapeDtypeStruct((z.modes, z.share), F32),
        jax.ShapeDtypeStruct((z.modes, z.share), F32),
    )
    results = pl.pallas_call(
        body,
        out_shape=shapes,
        in_specs=[any_spec] * 5 + [smem] * 3,
        out_specs=[any_spec] * 4,
        scratch_shapes=flat,
        cost_estimate=pl.CostEstimate(flops=flops, bytes_accessed=10_000_000, transcendentals=0),
        compiler_params=pltpu.CompilerParams(
            collective_id=0, has_side_effects=True, vmem_limit_bytes=58 * 1024 * 1024
        ),
    )(snaps_primal, snaps_adjoint, coef_primal, coef_adjoint, op_blocks, counts, col_index.T, ghost_send)
    return pl.pallas_call(
        hand_over,
        out_shape=shapes,
        in_specs=[pl.BlockSpec(memory_space=pltpu.VMEM)] * 4,
        out_specs=[any_spec] * 4,
        scratch_shapes=[pltpu.SemaphoreType.DMA((4,))],
    )(*results)


def solution(mesh):
    placed = (
        P("snap", "space"),
        P("snap", "space"),
        P("snap", None),
        P("snap", None),
        P("space", None, None, None),
        P("space"),
        P("space", None),
        P("space", None, None),
    )
    return jax.shard_map(
        per_device,
        mesh=mesh,
        in_specs=placed,
        out_specs=(P("snap", "space"), P("snap", "space"), P(None, "snap"), P(None, "snap")),
        check_vma=False,
    )
```

```python
import math

import jax
import jax.numpy as jnp
from jax import lax
from jax.experimental import pallas as pl
from jax.experimental.pallas import tpu as pltpu
from jax.sharding import PartitionSpec as P

MESH = pl.DeviceIdType.MESH
BF16 = jnp.bfloat16
F32 = jnp.float32
OFFSETS = (-2, -1, 1, 2)
TILE_BLOCKS = 4
CHUNKS = ((64,), (64,), (48, 48), (32,))


class Sizes:
    def __init__(self, n_space, n_snap, snaps, coef, op_blocks, ghost_send):
        self.n_space, self.n_snap = n_space, n_snap
        self.devices = n_space * n_snap
        self.snaps, self.unknowns = snaps.shape
        self.modes = coef.shape[1]
        self.share = self.modes // n_snap
        self.rows, self.slots, self.bs = op_blocks.shape[:3]
        self.lists, self.list_len = ghost_send.shape[1:]
        self.parts, self.sums, first = [], [], 0
        for g, sizes in enumerate(CHUNKS):
            self.sums.append((first, sum(sizes)))
            for size in sizes:
                self.parts.append((first, size, g))
                first += size
        assert first == self.modes
        self.chunks = len(self.parts)
        self.piece = max(16, self.modes // n_space)
        self.owners = self.modes // self.piece
        self.tiles = self.rows // TILE_BLOCKS
        self.factor = 1.0 / math.sqrt(self.unknowns * n_space)

    def groups(self, first, size):
        last = first + size
        found = []
        for x in range(self.n_snap):
            lo, hi = max(first, x * self.share), min(last, (x + 1) * self.share)
            if lo < hi:
                found.append((x, lo - x * self.share, lo - first, hi - lo))
        return found


def chunk_scratch(z, mc):
    b, bs = z.rows, z.bs
    return {
        "q": pltpu.VMEM((b, mc, bs), BF16),
        "qr": pltpu.VMEM((z.n_snap - 1, b, mc, bs), BF16),
        "own": pltpu.VMEM((b, mc, bs), BF16),
        "ext": pltpu.VMEM((b + z.lists * z.list_len, mc, bs), BF16),
        "snd": pltpu.VMEM((z.lists, z.list_len, mc, bs), BF16),
    }


def sum_scratch(z, mc):
    return {
        "d": pltpu.VMEM((z.owners, z.piece, 2 * mc), BF16),
        "rs": pltpu.VMEM((z.devices, z.piece, 2 * mc), BF16),
        "gs": pltpu.VMEM((z.piece, 2 * mc), F32),
        "gat": pltpu.VMEM((z.n_space, z.piece, 2 * mc), F32),
    }


def scratch_of(z):
    bs = z.bs
    sem = pltpu.SemaphoreType.DMA
    return {
        "sp": pltpu.VMEM((z.snaps, z.unknowns), BF16),
        "sa": pltpu.VMEM((z.snaps, z.unknowns), BF16),
        "cp": pltpu.VMEM((z.snaps, z.modes), BF16),
        "ca": pltpu.VMEM((z.snaps, z.modes), BF16),
        "op": pltpu.VMEM((z.rows, z.slots, bs, bs), BF16),
        "adjt": pltpu.VMEM((z.unknowns, z.modes), BF16),
        "opt": pltpu.VMEM((z.rows, z.slots * bs, bs), BF16),
        "vt": pltpu.VMEM((z.tiles, TILE_BLOCKS * z.slots * bs, z.modes), BF16),
        "po": pltpu.VMEM((z.share, z.unknowns), BF16),
        "ao": pltpu.VMEM((z.share, z.unknowns), BF16),
        "ro": pltpu.VMEM((z.modes, z.share), F32),
        "go": pltpu.VMEM((z.modes, z.share), F32),
        "store": sem((4,)),
        "cpt": pltpu.VMEM((z.modes, z.snaps), BF16),
        "load": sem((5,)),
        "q_s": sem((z.chunks, z.n_snap - 1)),
        "q_r": sem((z.chunks, z.n_snap - 1)),
        "g_s": sem((z.chunks, z.lists)),
        "g_r": sem((z.chunks, z.lists)),
        "rs_s": sem((len(z.sums),)),
        "rs_r": sem((len(z.sums),)),
        "ag_s": sem((len(z.sums),)),
        "ag_r": sem((len(z.sums),)),
        "chunk": [chunk_scratch(z, size) for _, size, _ in z.parts],
        "sum": [sum_scratch(z, size) for _, size in z.sums],
    }


def transposed(value):
    return value.astype(F32).T.astype(BF16)


def matmul(a, b):
    return jnp.dot(a, b, preferred_element_type=F32)


def loop(count, body):
    def step(i, carry):
        body(i)
        return carry

    lax.fori_loop(0, count, step, 0)


def kernel(z, sp_hbm, sa_hbm, cp_hbm, ca_hbm, op_hbm, counts, cols, ghosts,
           primal_out, applied_out, reduced_out, gram_out, s):
    space, snap = lax.axis_index("space"), lax.axis_index("snap")
    me = space * z.n_snap + snap
    bs = z.bs
    width = TILE_BLOCKS * bs

    loads = [
        pltpu.make_async_copy(source, s[name], s["load"].at[i])
        for i, (source, name) in enumerate(
            [(cp_hbm, "cp"), (sp_hbm, "sp"), (ca_hbm, "ca"), (sa_hbm, "sa"), (op_hbm, "op")]
        )
    ]
    for copy in loads[:2]:
        copy.start()

    barrier = pltpu.get_barrier_semaphore()

    def greet(i):
        other = lax.rem(me + 1 + i, z.devices)
        pl.semaphore_signal(
            barrier,
            inc=1,
            device_id=(lax.div(other, z.n_snap), lax.rem(other, z.n_snap)),
            device_id_type=MESH,
        )

    loop(z.devices - 1, greet)

    def columns(t):
        return pl.ds(pl.multiple_of(t * width, width), width)

    def project(c):
        first, mc, _ = z.parts[c]
        coef = s["cpt"][first:first + mc, :]
        q = s["chunk"][c]["q"]

        def tile(t):
            part = jnp.dot(coef, s["sp"][:, columns(t)], preferred_element_type=F32).astype(BF16)
            for i in range(TILE_BLOCKS):
                q[t * TILE_BLOCKS + i] = part[:, i * bs:(i + 1) * bs]

        loop(z.tiles, tile)

    def partial_copy(c, i):
        k = s["chunk"][c]
        return pltpu.make_async_remote_copy(
            src_ref=k["q"],
            dst_ref=k["qr"].at[i],
            send_sem=s["q_s"].at[c, i],
            recv_sem=s["q_r"].at[c, i],
            device_id=(space, lax.rem(snap + 1 + i, z.n_snap)),
            device_id_type=MESH,
        )

    def ghost_copy(c, d):
        k = s["chunk"][c]
        first = z.rows + d * z.list_len
        return pltpu.make_async_remote_copy(
            src_ref=k["snd"].at[d],
            dst_ref=k["ext"].at[pl.ds(first, z.list_len)],
            send_sem=s["g_s"].at[c, d],
            recv_sem=s["g_r"].at[c, d],
            device_id=(space - OFFSETS[d], snap),
            device_id_type=MESH,
        )

    def inside(position):
        return (position >= 0) & (position < z.n_space)

    def blocks_of(t):
        return [t * TILE_BLOCKS + i for i in range(TILE_BLOCKS)]

    def carry_operator(t):
        for i, b in enumerate(blocks_of(t)):
            live = counts[b]
            for j in range(z.slots):
                s["opt"][b, j * bs:(j + 1) * bs, :] = s["op"][b, j].T
            part = matmul(s["opt"][b], s["adjt"][pl.ds(pl.multiple_of(b * bs, bs), bs), :])
            for j in range(z.slots):
                value = part[j * bs:(j + 1) * bs]
                value = jnp.where(j < live, value, jnp.zeros_like(value)).astype(BF16)
                first = (i * z.slots + j) * bs
                s["vt"][t, first:first + bs, :] = value

    def own_modes(c):
        k = s["chunk"][c]
        first_mode, mc, g = z.parts[c]
        sum_first, sum_size = z.sums[g]
        shift = first_mode - sum_first
        for i in range(z.n_snap - 1):
            partial_copy(c, i).wait_recv()

        def tile(t):
            for b in blocks_of(t):
                total = k["q"][b].astype(F32)
                for i in range(z.n_snap - 1):
                    total = total + k["qr"][i, b].astype(F32)
                total = total.astype(BF16)
                k["own"][b] = total
                k["ext"][b] = total

        loop(z.tiles, tile)
        for d in range(z.lists):
            for t in range(z.list_len):
                k["snd"][d, t] = k["own"][ghosts[0, d, t]]

            @pl.when(inside(space - OFFSETS[d]))
            def _():
                ghost_copy(c, d).start()

            @pl.when(jnp.logical_not(inside(space + OFFSETS[d])))
            def _():
                first = z.rows + d * z.list_len
                k["ext"][first:first + z.list_len] = jnp.zeros((z.list_len, mc, bs), BF16)

        def gram(t, total):
            left = jnp.concatenate([k["own"][b] for b in blocks_of(t)], axis=1)
            return total + matmul(left, s["adjt"][columns(t), :])

        terms = lax.fori_loop(0, z.tiles, gram, jnp.zeros((mc, z.modes), F32)).T
        lane = sum_size + shift
        s["sum"][g]["d"][:, :, lane:lane + mc] = terms.astype(BF16).reshape(z.owners, z.piece, mc)

        for x, at, start, count in z.groups(first_mode, mc):
            @pl.when(snap == x)
            def _():
                def keep(t):
                    for b in blocks_of(t):
                        s["po"][at:at + count, pl.ds(pl.multiple_of(b * bs, bs), bs)] = k["own"][b, start:start + count, :]

                loop(z.tiles, keep)

    def terms_of(c):
        k = s["chunk"][c]
        first_mode, mc, g = z.parts[c]
        shift = first_mode - z.sums[g][0]
        for d in range(z.lists):
            @pl.when(inside(space + OFFSETS[d]))
            def _():
                ghost_copy(c, d).wait_recv()

        def tile(t, total):
            picked = [k["ext"][cols[j, b]] for b in blocks_of(t) for j in range(z.slots)]
            return total + matmul(jnp.concatenate(picked, axis=1), s["vt"][t])

        terms = lax.fori_loop(0, z.tiles, tile, jnp.zeros((mc, z.modes), F32)).T
        s["sum"][g]["d"][:, :, shift:shift + mc] = terms.astype(BF16).reshape(z.owners, z.piece, mc)

    def share_out(g):
        k = s["sum"][g]
        for x, _, _, _ in z.groups(*z.sums[g]):
            def send(i):
                o = lax.rem(space + 1 + i, z.owners)
                same = (space == o) & (snap == x)

                @pl.when(same)
                def _():
                    k["rs"][me] = k["d"][o]

                @pl.when(jnp.logical_not(same))
                def _():
                    pltpu.make_async_remote_copy(
                        src_ref=k["d"].at[o],
                        dst_ref=k["rs"].at[me],
                        send_sem=s["rs_s"].at[g],
                        recv_sem=s["rs_r"].at[g],
                        device_id=(o, x),
                        device_id_type=MESH,
                    ).start()

            loop(z.owners, send)

    def apply(c, low, high):
        k = s["chunk"][c]
        for x, at, start, count in z.groups(*z.parts[c][:2]):
            @pl.when(snap == x)
            def _():
                def tile(t):
                    for b in blocks_of(low + t):
                        live = counts[b]
                        picked = []
                        for j in range(z.slots):
                            value = k["ext"][cols[j, b]][start:start + count]
                            picked.append(jnp.where(j < live, value, jnp.zeros_like(value)))
                        result = matmul(jnp.concatenate(picked, axis=1), s["opt"][b])
                        s["ao"][at:at + count, pl.ds(pl.multiple_of(b * bs, bs), bs)] = result.astype(BF16)

                loop(high - low, tile)

    def settle(ref, count, sem):
        part = ref.at[pl.ds(0, count)]
        pltpu.make_async_copy(part, part, sem).wait()

    def among(g):
        found = snap == z.groups(*z.sums[g])[0][0]
        for x, _, _, _ in z.groups(*z.sums[g])[1:]:
            found = found | (snap == x)
        return found

    def add_up(g):
        k = s["sum"][g]
        mc = z.sums[g][1]

        @pl.when(among(g) & (space < z.owners))
        def _():
            settle(k["rs"], z.devices - 1, s["rs_r"].at[g])
            total = lax.fori_loop(
                0,
                z.devices // 16,
                lambda i, t: t + jnp.sum(k["rs"][pl.ds(i * 16, 16)].astype(F32), axis=0),
                jnp.zeros((z.piece, 2 * mc), F32),
            )
            total = total * z.factor
            k["gs"][...] = total
            k["gat"][space] = total

            def send(i):
                pltpu.make_async_remote_copy(
                    src_ref=k["gs"],
                    dst_ref=k["gat"].at[space],
                    send_sem=s["ag_s"].at[g],
                    recv_sem=s["ag_r"].at[g],
                    device_id=(lax.rem(space + 1 + i, z.n_space), snap),
                    device_id_type=MESH,
                ).start()

            loop(z.n_space - 1, send)

    def finish(g):
        k = s["sum"][g]
        mc = z.sums[g][1]
        for x, at, start, count in z.groups(*z.sums[g]):
            @pl.when(snap == x)
            def _():
                @pl.when(space < z.owners)
                def _():
                    settle(k["gat"], z.owners - 1, s["ag_r"].at[g])

                if z.owners < z.n_space:
                    @pl.when(space >= z.owners)
                    def _():
                        settle(k["gat"], z.owners, s["ag_r"].at[g])

                whole = k["gat"][:z.owners].reshape(z.modes, 2 * mc)
                s["ro"][:, at:at + count] = whole[:, start:start + count]
                s["go"][:, at:at + count] = whole[:, mc + start:mc + start + count]

    loads[0].wait()
    s["cpt"][...] = transposed(s["cp"][...])
    loads[1].wait()
    for copy in loads[2:]:
        copy.start()
    project(0)
    pl.semaphore_wait(barrier, z.devices - 1)
    for c in range(z.chunks):
        if c:
            project(c)
        for i in range(z.n_snap - 1):
            partial_copy(c, i).start()

    loads[2].wait()
    cat = transposed(s["ca"][...])
    loads[3].wait()

    def adjoint(t):
        s["adjt"][columns(t), :] = matmul(cat, s["sa"][:, columns(t)]).T.astype(BF16)

    loop(z.tiles, adjoint)
    loads[4].wait()
    loop(z.tiles, carry_operator)

    stores = [
        pltpu.make_async_copy(s[name], target, s["store"].at[i])
        for i, (name, target) in enumerate(
            [("po", primal_out), ("ao", applied_out), ("ro", reduced_out), ("go", gram_out)]
        )
    ]
    last = z.chunks - 1

    def ends(c):
        return c == last or z.parts[c + 1][2] != z.parts[c][2]

    def reduced_terms(c):
        terms_of(c)
        if ends(c):
            share_out(z.parts[c][2])

    pending = []
    for c in range(z.chunks):
        own_modes(c)
        if c == last:
            stores[0].start()
        if c:
            reduced_terms(c - 1)
            if c < last:
                apply(c - 1, 0, z.tiles)
                for g in pending:
                    add_up(g)
                pending = [z.parts[c - 1][2]] if ends(c - 1) else []
            elif ends(c - 1):
                pending.append(z.parts[c - 1][2])
    reduced_terms(last)
    for g in pending:
        add_up(g)
    apply(last - 1, 0, z.tiles)
    add_up(z.parts[last][2])
    apply(last, 0, z.tiles)
    stores[1].start()
    for g in range(len(z.sums)):
        finish(g)
    stores[2].start()
    stores[3].start()

    for c in range(z.chunks):
        for i in range(z.n_snap - 1):
            partial_copy(c, i).wait_send()
        for d in range(z.lists):
            @pl.when(inside(space - OFFSETS[d]))
            def _():
                ghost_copy(c, d).wait_send()

    for g in range(len(z.sums)):
        k = s["sum"][g]
        count = len(z.groups(*z.sums[g])) * z.owners
        owner = among(g) & (space < z.owners)

        @pl.when(owner)
        def _():
            settle(k["rs"], count - 1, s["rs_s"].at[g])
            settle(k["gat"], z.n_space - 1, s["ag_s"].at[g])

        @pl.when(jnp.logical_not(owner))
        def _():
            settle(k["rs"], count, s["rs_s"].at[g])

    for copy in stores:
        copy.wait()


def hand_over(*refs):
    copies = [pltpu.make_async_copy(refs[i], refs[4 + i], refs[8].at[i]) for i in range(4)]
    for copy in copies:
        copy.start()
    for copy in copies:
        copy.wait()


def per_device(
    snaps_primal, snaps_adjoint, coef_primal, coef_adjoint, op_blocks, counts, col_index, ghost_send
):
    z = Sizes(
        lax.axis_size("space"), lax.axis_size("snap"), snaps_primal, coef_primal, op_blocks, ghost_send
    )
    any_spec = pl.BlockSpec(memory_space=pl.ANY)
    smem = pl.BlockSpec(memory_space=pltpu.SMEM)
    names = scratch_of(z)
    flat, tree = jax.tree.flatten(names)

    def body(*refs):
        s = jax.tree.unflatten(tree, refs[12:])
        kernel(z, *refs[:12], s)

    flops = 2 * z.unknowns * z.modes * (2 * z.snaps + z.slots * z.bs + 2 * z.modes)
    shapes = (
        jax.ShapeDtypeStruct((z.share, z.unknowns), BF16),
        jax.ShapeDtypeStruct((z.share, z.unknowns), BF16),
        jax.ShapeDtypeStruct((z.modes, z.share), F32),
        jax.ShapeDtypeStruct((z.modes, z.share), F32),
    )
    results = pl.pallas_call(
        body,
        out_shape=shapes,
        in_specs=[any_spec] * 5 + [smem] * 3,
        out_specs=[any_spec] * 4,
        scratch_shapes=flat,
        cost_estimate=pl.CostEstimate(flops=flops, bytes_accessed=10_000_000, transcendentals=0),
        compiler_params=pltpu.CompilerParams(
            collective_id=0, has_side_effects=True, vmem_limit_bytes=58 * 1024 * 1024
        ),
    )(snaps_primal, snaps_adjoint, coef_primal, coef_adjoint, op_blocks, counts, col_index.T, ghost_send)
    return pl.pallas_call(
        hand_over,
        out_shape=shapes,
        in_specs=[pl.BlockSpec(memory_space=pltpu.VMEM)] * 4,
        out_specs=[any_spec] * 4,
        scratch_shapes=[pltpu.SemaphoreType.DMA((4,))],
    )(*results)


def solution(mesh):
    placed = (
        P("snap", "space"),
        P("snap", "space"),
        P("snap", None),
        P("snap", None),
        P("space", None, None, None),
        P("space"),
        P("space", None),
        P("space", None, None),
    )
    return jax.shard_map(
        per_device,
        mesh=mesh,
        in_specs=placed,
        out_specs=(P("snap", "space"), P("snap", "space"), P(None, "snap"), P(None, "snap")),
        check_vma=False,
    )
```

```python
import math

import jax
import jax.numpy as jnp
from jax import lax
from jax.experimental import pallas as pl
from jax.experimental.pallas import tpu as pltpu
from jax.sharding import PartitionSpec as P

MESH = pl.DeviceIdType.MESH
BF16 = jnp.bfloat16
F32 = jnp.float32
OFFSETS = (-2, -1, 1, 2)
TILE_BLOCKS = 4
CHUNKS = ((64,), (64,), (64,), (32, 32))


class Sizes:
    def __init__(self, n_space, n_snap, snaps, coef, op_blocks, ghost_send):
        self.n_space, self.n_snap = n_space, n_snap
        self.devices = n_space * n_snap
        self.snaps, self.unknowns = snaps.shape
        self.modes = coef.shape[1]
        self.share = self.modes // n_snap
        self.rows, self.slots, self.bs = op_blocks.shape[:3]
        self.lists, self.list_len = ghost_send.shape[1:]
        self.parts, self.sums, first = [], [], 0
        for g, sizes in enumerate(CHUNKS):
            self.sums.append((first, sum(sizes)))
            for size in sizes:
                self.parts.append((first, size, g))
                first += size
        assert first == self.modes
        self.chunks = len(self.parts)
        self.piece = max(16, self.modes // n_space)
        self.owners = self.modes // self.piece
        self.tiles = self.rows // TILE_BLOCKS
        self.factor = 1.0 / math.sqrt(self.unknowns * n_space)

    def groups(self, first, size):
        last = first + size
        found = []
        for x in range(self.n_snap):
            lo, hi = max(first, x * self.share), min(last, (x + 1) * self.share)
            if lo < hi:
                found.append((x, lo - x * self.share, lo - first, hi - lo))
        return found


def chunk_scratch(z, mc):
    b, bs = z.rows, z.bs
    return {
        "q": pltpu.VMEM((b, mc, bs), BF16),
        "qr": pltpu.VMEM((z.n_snap - 1, b, mc, bs), BF16),
        "own": pltpu.VMEM((b, mc, bs), BF16),
        "ext": pltpu.VMEM((b + z.lists * z.list_len, mc, bs), BF16),
        "snd": pltpu.VMEM((z.lists, z.list_len, mc, bs), BF16),
    }


def sum_scratch(z, mc):
    return {
        "d": pltpu.VMEM((z.owners, z.piece, 2 * mc), BF16),
        "rs": pltpu.VMEM((z.devices, z.piece, 2 * mc), BF16),
        "gs": pltpu.VMEM((z.piece, 2 * mc), BF16),
        "gat": pltpu.VMEM((z.n_space, z.piece, 2 * mc), BF16),
    }


def scratch_of(z):
    bs = z.bs
    sem = pltpu.SemaphoreType.DMA
    return {
        "sp": pltpu.VMEM((z.snaps, z.unknowns), BF16),
        "sa": pltpu.VMEM((z.snaps, z.unknowns), BF16),
        "cp": pltpu.VMEM((z.snaps, z.modes), BF16),
        "ca": pltpu.VMEM((z.snaps, z.modes), BF16),
        "op": pltpu.VMEM((z.rows, z.slots, bs, bs), BF16),
        "adjt": pltpu.VMEM((z.unknowns, z.modes), BF16),
        "opt": pltpu.VMEM((z.rows, z.slots * bs, bs), BF16),
        "vt": pltpu.VMEM((z.tiles, TILE_BLOCKS * z.slots * bs, z.modes), BF16),
        "po": pltpu.VMEM((z.share, z.unknowns), BF16),
        "ao": pltpu.VMEM((z.share, z.unknowns), BF16),
        "ro": pltpu.VMEM((z.modes, z.share), F32),
        "go": pltpu.VMEM((z.modes, z.share), F32),
        "store": sem((4,)),
        "cpt": pltpu.VMEM((z.modes, z.snaps), BF16),
        "load": sem((5,)),
        "q_s": sem((z.chunks, z.n_snap - 1, 2)),
        "q_r": sem((z.chunks, z.n_snap - 1, 2)),
        "g_s": sem((z.chunks, z.lists)),
        "g_r": sem((z.chunks, z.lists)),
        "rs_s": sem((len(z.sums),)),
        "rs_r": sem((len(z.sums),)),
        "ag_s": sem((len(z.sums),)),
        "ag_r": sem((len(z.sums),)),
        "chunk": [chunk_scratch(z, size) for _, size, _ in z.parts],
        "sum": [sum_scratch(z, size) for _, size in z.sums],
    }


def transposed(value):
    return value.astype(F32).T.astype(BF16)


def matmul(a, b):
    return jnp.dot(a, b, preferred_element_type=F32)


def loop(count, body):
    def step(i, carry):
        body(i)
        return carry

    lax.fori_loop(0, count, step, 0)


def kernel(z, sp_hbm, sa_hbm, cp_hbm, ca_hbm, op_hbm, counts, cols, ghosts,
           primal_out, applied_out, reduced_out, gram_out, s):
    space, snap = lax.axis_index("space"), lax.axis_index("snap")
    me = space * z.n_snap + snap
    bs = z.bs
    width = TILE_BLOCKS * bs

    loads = [
        pltpu.make_async_copy(source, s[name], s["load"].at[i])
        for i, (source, name) in enumerate(
            [(cp_hbm, "cp"), (sp_hbm, "sp"), (ca_hbm, "ca"), (sa_hbm, "sa"), (op_hbm, "op")]
        )
    ]
    for copy in loads[:2]:
        copy.start()

    barrier = pltpu.get_barrier_semaphore()

    def greet(i):
        other = lax.rem(me + 1 + i, z.devices)
        pl.semaphore_signal(
            barrier,
            inc=1,
            device_id=(lax.div(other, z.n_snap), lax.rem(other, z.n_snap)),
            device_id_type=MESH,
        )

    loop(z.devices - 1, greet)

    def columns(t):
        return pl.ds(pl.multiple_of(t * width, width), width)

    def project(c):
        first, mc, _ = z.parts[c]
        coef = s["cpt"][first:first + mc, :]
        q = s["chunk"][c]["q"]

        def tile(t):
            part = jnp.dot(coef, s["sp"][:, columns(t)], preferred_element_type=F32).astype(BF16)
            for i in range(TILE_BLOCKS):
                q[t * TILE_BLOCKS + i] = part[:, i * bs:(i + 1) * bs]

        loop(z.tiles, tile)

    def partial_copy(c, i, h):
        k = s["chunk"][c]
        half = z.rows // 2
        return pltpu.make_async_remote_copy(
            src_ref=k["q"].at[pl.ds(h * half, half)],
            dst_ref=k["qr"].at[i, pl.ds(h * half, half)],
            send_sem=s["q_s"].at[c, i, h],
            recv_sem=s["q_r"].at[c, i, h],
            device_id=(space, lax.rem(snap + 1 + i, z.n_snap)),
            device_id_type=MESH,
        )

    def ghost_copy(c, d):
        k = s["chunk"][c]
        first = z.rows + d * z.list_len
        return pltpu.make_async_remote_copy(
            src_ref=k["snd"].at[d],
            dst_ref=k["ext"].at[pl.ds(first, z.list_len)],
            send_sem=s["g_s"].at[c, d],
            recv_sem=s["g_r"].at[c, d],
            device_id=(space - OFFSETS[d], snap),
            device_id_type=MESH,
        )

    def inside(position):
        return (position >= 0) & (position < z.n_space)

    def blocks_of(t):
        return [t * TILE_BLOCKS + i for i in range(TILE_BLOCKS)]

    def carry_operator(t):
        for i, b in enumerate(blocks_of(t)):
            live = counts[b]
            for j in range(z.slots):
                s["opt"][b, j * bs:(j + 1) * bs, :] = s["op"][b, j].T
            part = matmul(s["opt"][b], s["adjt"][pl.ds(pl.multiple_of(b * bs, bs), bs), :])
            for j in range(z.slots):
                value = part[j * bs:(j + 1) * bs]
                value = jnp.where(j < live, value, jnp.zeros_like(value)).astype(BF16)
                first = (i * z.slots + j) * bs
                s["vt"][t, first:first + bs, :] = value

    def own_modes(c):
        k = s["chunk"][c]
        first_mode, mc, g = z.parts[c]
        sum_first, sum_size = z.sums[g]
        shift = first_mode - sum_first
        for h in range(2):
            for i in range(z.n_snap - 1):
                partial_copy(c, i, h).wait()
                if c + 1 < z.chunks:
                    partial_copy(c + 1, i, h).start()

        def tile(t):
            for b in blocks_of(t):
                total = k["q"][b].astype(F32)
                for i in range(z.n_snap - 1):
                    total = total + k["qr"][i, b].astype(F32)
                total = total.astype(BF16)
                k["own"][b] = total
                k["ext"][b] = total

        loop(z.tiles, tile)
        for d in range(z.lists):
            for t in range(z.list_len):
                k["snd"][d, t] = k["own"][ghosts[0, d, t]]

            @pl.when(inside(space - OFFSETS[d]))
            def _():
                ghost_copy(c, d).start()

            @pl.when(jnp.logical_not(inside(space + OFFSETS[d])))
            def _():
                first = z.rows + d * z.list_len
                k["ext"][first:first + z.list_len] = jnp.zeros((z.list_len, mc, bs), BF16)

        def gram(t, total):
            left = jnp.concatenate([k["own"][b] for b in blocks_of(t)], axis=1)
            return total + matmul(left, s["adjt"][columns(t), :])

        terms = lax.fori_loop(0, z.tiles, gram, jnp.zeros((mc, z.modes), F32)).T
        lane = sum_size + shift
        s["sum"][g]["d"][:, :, lane:lane + mc] = terms.astype(BF16).reshape(z.owners, z.piece, mc)

        for x, at, start, count in z.groups(first_mode, mc):
            @pl.when(snap == x)
            def _():
                def keep(t):
                    for b in blocks_of(t):
                        s["po"][at:at + count, pl.ds(pl.multiple_of(b * bs, bs), bs)] = k["own"][b, start:start + count, :]

                loop(z.tiles, keep)

    def terms_of(c):
        k = s["chunk"][c]
        first_mode, mc, g = z.parts[c]
        shift = first_mode - z.sums[g][0]
        for d in range(z.lists):
            @pl.when(inside(space + OFFSETS[d]))
            def _():
                ghost_copy(c, d).wait_recv()

        def tile(t, total):
            picked = [k["ext"][cols[j, b]] for b in blocks_of(t) for j in range(z.slots)]
            return total + matmul(jnp.concatenate(picked, axis=1), s["vt"][t])

        terms = lax.fori_loop(0, z.tiles, tile, jnp.zeros((mc, z.modes), F32)).T
        s["sum"][g]["d"][:, :, shift:shift + mc] = terms.astype(BF16).reshape(z.owners, z.piece, mc)

    def share_out(g):
        k = s["sum"][g]
        for x, _, _, _ in z.groups(*z.sums[g]):
            def send(i):
                o = lax.rem(space + 1 + i, z.owners)
                same = (space == o) & (snap == x)

                @pl.when(same)
                def _():
                    k["rs"][me] = k["d"][o]

                @pl.when(jnp.logical_not(same))
                def _():
                    pltpu.make_async_remote_copy(
                        src_ref=k["d"].at[o],
                        dst_ref=k["rs"].at[me],
                        send_sem=s["rs_s"].at[g],
                        recv_sem=s["rs_r"].at[g],
                        device_id=(o, x),
                        device_id_type=MESH,
                    ).start()

            loop(z.owners, send)

    def apply(c, low, high):
        k = s["chunk"][c]
        for x, at, start, count in z.groups(*z.parts[c][:2]):
            @pl.when(snap == x)
            def _():
                def tile(t):
                    for b in blocks_of(low + t):
                        live = counts[b]
                        picked = []
                        for j in range(z.slots):
                            value = k["ext"][cols[j, b]][start:start + count]
                            picked.append(jnp.where(j < live, value, jnp.zeros_like(value)))
                        result = matmul(jnp.concatenate(picked, axis=1), s["opt"][b])
                        s["ao"][at:at + count, pl.ds(pl.multiple_of(b * bs, bs), bs)] = result.astype(BF16)

                loop(high - low, tile)

    def settle(ref, count, sem):
        part = ref.at[pl.ds(0, count)]
        pltpu.make_async_copy(part, part, sem).wait()

    def among(g):
        found = snap == z.groups(*z.sums[g])[0][0]
        for x, _, _, _ in z.groups(*z.sums[g])[1:]:
            found = found | (snap == x)
        return found

    def add_up(g):
        k = s["sum"][g]
        mc = z.sums[g][1]

        @pl.when(among(g) & (space < z.owners))
        def _():
            settle(k["rs"], z.devices - 1, s["rs_r"].at[g])
            total = lax.fori_loop(
                0,
                z.devices // 16,
                lambda i, t: t + jnp.sum(k["rs"][pl.ds(i * 16, 16)].astype(F32), axis=0),
                jnp.zeros((z.piece, 2 * mc), F32),
            )
            total = (total * z.factor).astype(BF16)
            k["gs"][...] = total
            k["gat"][space] = total

            def send(i):
                pltpu.make_async_remote_copy(
                    src_ref=k["gs"],
                    dst_ref=k["gat"].at[space],
                    send_sem=s["ag_s"].at[g],
                    recv_sem=s["ag_r"].at[g],
                    device_id=(lax.rem(space + 1 + i, z.n_space), snap),
                    device_id_type=MESH,
                ).start()

            loop(z.n_space - 1, send)

    def finish(g):
        k = s["sum"][g]
        mc = z.sums[g][1]
        for x, at, start, count in z.groups(*z.sums[g]):
            @pl.when(snap == x)
            def _():
                @pl.when(space < z.owners)
                def _():
                    settle(k["gat"], z.owners - 1, s["ag_r"].at[g])

                if z.owners < z.n_space:
                    @pl.when(space >= z.owners)
                    def _():
                        settle(k["gat"], z.owners, s["ag_r"].at[g])

                whole = k["gat"][:z.owners].astype(F32).reshape(z.modes, 2 * mc)
                s["ro"][:, at:at + count] = whole[:, start:start + count]
                s["go"][:, at:at + count] = whole[:, mc + start:mc + start + count]

    loads[0].wait()
    s["cpt"][...] = transposed(s["cp"][...])
    loads[1].wait()
    for copy in loads[2:]:
        copy.start()
    project(0)
    pl.semaphore_wait(barrier, z.devices - 1)
    for h in range(2):
        for i in range(z.n_snap - 1):
            partial_copy(0, i, h).start()
    for c in range(1, z.chunks):
        project(c)

    loads[2].wait()
    cat = transposed(s["ca"][...])
    loads[3].wait()

    def adjoint(t):
        s["adjt"][columns(t), :] = matmul(cat, s["sa"][:, columns(t)]).T.astype(BF16)

    loop(z.tiles, adjoint)
    loads[4].wait()
    loop(z.tiles, carry_operator)

    stores = [
        pltpu.make_async_copy(s[name], target, s["store"].at[i])
        for i, (name, target) in enumerate(
            [("po", primal_out), ("ao", applied_out), ("ro", reduced_out), ("go", gram_out)]
        )
    ]
    last = z.chunks - 1

    def ends(c):
        return c == last or z.parts[c + 1][2] != z.parts[c][2]

    def reduced_terms(c):
        terms_of(c)
        if ends(c):
            share_out(z.parts[c][2])

    pending = []
    for c in range(z.chunks):
        own_modes(c)
        if c == last:
            stores[0].start()
        for g in pending:
            add_up(g)
        pending = []
        if c:
            reduced_terms(c - 1)
            if ends(c - 1):
                pending = [z.parts[c - 1][2]]
            if c < last:
                apply(c - 1, 0, z.tiles)
    reduced_terms(last)
    for g in pending:
        add_up(g)
    apply(last - 1, 0, z.tiles)
    add_up(z.parts[last][2])
    apply(last, 0, z.tiles)
    stores[1].start()
    for g in range(len(z.sums)):
        finish(g)
    stores[2].start()
    stores[3].start()

    for c in range(z.chunks):
        for d in range(z.lists):
            @pl.when(inside(space - OFFSETS[d]))
            def _():
                ghost_copy(c, d).wait_send()

    for g in range(len(z.sums)):
        k = s["sum"][g]
        count = len(z.groups(*z.sums[g])) * z.owners
        owner = among(g) & (space < z.owners)

        @pl.when(owner)
        def _():
            settle(k["rs"], count - 1, s["rs_s"].at[g])
            settle(k["gat"], z.n_space - 1, s["ag_s"].at[g])

        @pl.when(jnp.logical_not(owner))
        def _():
            settle(k["rs"], count, s["rs_s"].at[g])

    for copy in stores:
        copy.wait()


def hand_over(*refs):
    copies = [pltpu.make_async_copy(refs[i], refs[4 + i], refs[8].at[i]) for i in range(4)]
    for copy in copies:
        copy.start()
    for copy in copies:
        copy.wait()


def per_device(
    snaps_primal, snaps_adjoint, coef_primal, coef_adjoint, op_blocks, counts, col_index, ghost_send
):
    z = Sizes(
        lax.axis_size("space"), lax.axis_size("snap"), snaps_primal, coef_primal, op_blocks, ghost_send
    )
    any_spec = pl.BlockSpec(memory_space=pl.ANY)
    smem = pl.BlockSpec(memory_space=pltpu.SMEM)
    names = scratch_of(z)
    flat, tree = jax.tree.flatten(names)

    def body(*refs):
        s = jax.tree.unflatten(tree, refs[12:])
        kernel(z, *refs[:12], s)

    flops = 2 * z.unknowns * z.modes * (2 * z.snaps + z.slots * z.bs + 2 * z.modes)
    shapes = (
        jax.ShapeDtypeStruct((z.share, z.unknowns), BF16),
        jax.ShapeDtypeStruct((z.share, z.unknowns), BF16),
        jax.ShapeDtypeStruct((z.modes, z.share), F32),
        jax.ShapeDtypeStruct((z.modes, z.share), F32),
    )
    results = pl.pallas_call(
        body,
        out_shape=shapes,
        in_specs=[any_spec] * 5 + [smem] * 3,
        out_specs=[any_spec] * 4,
        scratch_shapes=flat,
        cost_estimate=pl.CostEstimate(flops=flops, bytes_accessed=10_000_000, transcendentals=0),
        compiler_params=pltpu.CompilerParams(
            collective_id=0, has_side_effects=True, vmem_limit_bytes=58 * 1024 * 1024
        ),
    )(snaps_primal, snaps_adjoint, coef_primal, coef_adjoint, op_blocks, counts, col_index.T, ghost_send)
    return pl.pallas_call(
        hand_over,
        out_shape=shapes,
        in_specs=[pl.BlockSpec(memory_space=pltpu.VMEM)] * 4,
        out_specs=[any_spec] * 4,
        scratch_shapes=[pltpu.SemaphoreType.DMA((4,))],
    )(*results)


def solution(mesh):
    placed = (
        P("snap", "space"),
        P("snap", "space"),
        P("snap", None),
        P("snap", None),
        P("space", None, None, None),
        P("space"),
        P("space", None),
        P("space", None, None),
    )
    return jax.shard_map(
        per_device,
        mesh=mesh,
        in_specs=placed,
        out_specs=(P("snap", "space"), P("snap", "space"), P(None, "snap"), P(None, "snap")),
        check_vma=False,
    )
```

```python
import math

import jax
import jax.numpy as jnp
from jax import lax
from jax.experimental import pallas as pl
from jax.experimental.pallas import tpu as pltpu
from jax.sharding import PartitionSpec as P

MESH = pl.DeviceIdType.MESH
BF16 = jnp.bfloat16
F32 = jnp.float32
OFFSETS = (-2, -1, 1, 2)
TILE_BLOCKS = 4
CHUNKS = ((64,), (64,), (64,), (32, 32))


class Sizes:
    def __init__(self, n_space, n_snap, snaps, coef, op_blocks, ghost_send):
        self.n_space, self.n_snap = n_space, n_snap
        self.devices = n_space * n_snap
        self.snaps, self.unknowns = snaps.shape
        self.modes = coef.shape[1]
        self.share = self.modes // n_snap
        self.rows, self.slots, self.bs = op_blocks.shape[:3]
        self.lists, self.list_len = ghost_send.shape[1:]
        self.parts, self.sums, first = [], [], 0
        for g, sizes in enumerate(CHUNKS):
            self.sums.append((first, sum(sizes)))
            for size in sizes:
                self.parts.append((first, size, g))
                first += size
        assert first == self.modes
        self.chunks = len(self.parts)
        self.piece = max(16, self.modes // n_space)
        self.owners = self.modes // self.piece
        self.tiles = self.rows // TILE_BLOCKS
        self.factor = 1.0 / math.sqrt(self.unknowns * n_space)

    def groups(self, first, size):
        last = first + size
        found = []
        for x in range(self.n_snap):
            lo, hi = max(first, x * self.share), min(last, (x + 1) * self.share)
            if lo < hi:
                found.append((x, lo - x * self.share, lo - first, hi - lo))
        return found


def chunk_scratch(z, mc):
    b, bs = z.rows, z.bs
    return {
        "q": pltpu.VMEM((b, mc, bs), BF16),
        "qr": pltpu.VMEM((z.n_snap - 1, b, mc, bs), BF16),
        "own": pltpu.VMEM((b, mc, bs), BF16),
        "ext": pltpu.VMEM((b + z.lists * z.list_len, mc, bs), BF16),
        "snd": pltpu.VMEM((z.lists, z.list_len, mc, bs), BF16),
    }


def sum_scratch(z, mc, near):
    return {
        "pt": pltpu.VMEM((z.piece, 2 * mc), F32),
        "ps": pltpu.VMEM((z.n_snap - 1, z.piece, 2 * mc), F32),
        "d": pltpu.VMEM((z.owners, z.piece, 2 * mc), BF16),
        "rs": pltpu.VMEM((z.n_space if near else z.devices, z.piece, 2 * mc), BF16),
        "gs": pltpu.VMEM((z.piece, 2 * mc), BF16),
        "gat": pltpu.VMEM((z.n_space, z.piece, 2 * mc), BF16),
    }


def scratch_of(z):
    bs = z.bs
    sem = pltpu.SemaphoreType.DMA
    return {
        "sp": pltpu.VMEM((z.snaps, z.unknowns), BF16),
        "sa": pltpu.VMEM((z.snaps, z.unknowns), BF16),
        "cp": pltpu.VMEM((z.snaps, z.modes), BF16),
        "ca": pltpu.VMEM((z.snaps, z.modes), BF16),
        "op": pltpu.VMEM((z.rows, z.slots, bs, bs), BF16),
        "adjt": pltpu.VMEM((z.unknowns, z.modes), BF16),
        "opt": pltpu.VMEM((z.rows, z.slots * bs, bs), BF16),
        "vt": pltpu.VMEM((z.tiles, TILE_BLOCKS * z.slots * bs, z.modes), BF16),
        "po": pltpu.VMEM((z.share, z.unknowns), BF16),
        "ao": pltpu.VMEM((z.share, z.unknowns), BF16),
        "ro": pltpu.VMEM((z.modes, z.share), F32),
        "go": pltpu.VMEM((z.modes, z.share), F32),
        "store": sem((4,)),
        "cpt": pltpu.VMEM((z.modes, z.snaps), BF16),
        "load": sem((5,)),
        "q_s": sem((z.chunks, z.n_snap - 1, 2)),
        "q_r": sem((z.chunks, z.n_snap - 1, 2)),
        "g_s": sem((z.chunks, z.lists)),
        "g_r": sem((z.chunks, z.lists)),
        "rs_s": sem((len(z.sums),)),
        "rs_r": sem((len(z.sums),)),
        "ps_s": sem((len(z.sums),)),
        "ps_r": sem((len(z.sums),)),
        "ag_s": sem((len(z.sums),)),
        "ag_r": sem((len(z.sums),)),
        "chunk": [chunk_scratch(z, size) for _, size, _ in z.parts],
        "sum": [sum_scratch(z, size, g + 1 < len(z.sums)) for g, (_, size) in enumerate(z.sums)],
    }


def transposed(value):
    return value.astype(F32).T.astype(BF16)


def matmul(a, b):
    return jnp.dot(a, b, preferred_element_type=F32)


def loop(count, body):
    def step(i, carry):
        body(i)
        return carry

    lax.fori_loop(0, count, step, 0)


def kernel(z, sp_hbm, sa_hbm, cp_hbm, ca_hbm, op_hbm, counts, cols, ghosts,
           primal_out, applied_out, reduced_out, gram_out, s):
    space, snap = lax.axis_index("space"), lax.axis_index("snap")
    me = space * z.n_snap + snap
    bs = z.bs
    width = TILE_BLOCKS * bs

    loads = [
        pltpu.make_async_copy(source, s[name], s["load"].at[i])
        for i, (source, name) in enumerate(
            [(cp_hbm, "cp"), (sp_hbm, "sp"), (ca_hbm, "ca"), (sa_hbm, "sa"), (op_hbm, "op")]
        )
    ]
    for copy in loads[:2]:
        copy.start()

    barrier = pltpu.get_barrier_semaphore()

    def greet(i):
        other = lax.rem(me + 1 + i, z.devices)
        pl.semaphore_signal(
            barrier,
            inc=1,
            device_id=(lax.div(other, z.n_snap), lax.rem(other, z.n_snap)),
            device_id_type=MESH,
        )

    loop(z.devices - 1, greet)

    def columns(t):
        return pl.ds(pl.multiple_of(t * width, width), width)

    def project(c):
        first, mc, _ = z.parts[c]
        coef = s["cpt"][first:first + mc, :]
        q = s["chunk"][c]["q"]

        def tile(t):
            part = jnp.dot(coef, s["sp"][:, columns(t)], preferred_element_type=F32).astype(BF16)
            for i in range(TILE_BLOCKS):
                q[t * TILE_BLOCKS + i] = part[:, i * bs:(i + 1) * bs]

        loop(z.tiles, tile)

    def partial_copy(c, i, h):
        k = s["chunk"][c]
        half = z.rows // 2
        return pltpu.make_async_remote_copy(
            src_ref=k["q"].at[pl.ds(h * half, half)],
            dst_ref=k["qr"].at[i, pl.ds(h * half, half)],
            send_sem=s["q_s"].at[c, i, h],
            recv_sem=s["q_r"].at[c, i, h],
            device_id=(space, lax.rem(snap + 1 + i, z.n_snap)),
            device_id_type=MESH,
        )

    def ghost_copy(c, d):
        k = s["chunk"][c]
        first = z.rows + d * z.list_len
        return pltpu.make_async_remote_copy(
            src_ref=k["snd"].at[d],
            dst_ref=k["ext"].at[pl.ds(first, z.list_len)],
            send_sem=s["g_s"].at[c, d],
            recv_sem=s["g_r"].at[c, d],
            device_id=(space - OFFSETS[d], snap),
            device_id_type=MESH,
        )

    def inside(position):
        return (position >= 0) & (position < z.n_space)

    def blocks_of(t):
        return [t * TILE_BLOCKS + i for i in range(TILE_BLOCKS)]

    def carry_operator(t):
        for i, b in enumerate(blocks_of(t)):
            live = counts[b]
            for j in range(z.slots):
                s["opt"][b, j * bs:(j + 1) * bs, :] = s["op"][b, j].T
            part = matmul(s["opt"][b], s["adjt"][pl.ds(pl.multiple_of(b * bs, bs), bs), :])
            for j in range(z.slots):
                value = part[j * bs:(j + 1) * bs]
                value = jnp.where(j < live, value, jnp.zeros_like(value)).astype(BF16)
                first = (i * z.slots + j) * bs
                s["vt"][t, first:first + bs, :] = value

    def own_modes(c):
        k = s["chunk"][c]
        first_mode, mc, g = z.parts[c]
        sum_first, sum_size = z.sums[g]
        shift = first_mode - sum_first
        for h in range(2):
            for i in range(z.n_snap - 1):
                partial_copy(c, i, h).wait()
                if c + 1 < z.chunks:
                    partial_copy(c + 1, i, h).start()

        def tile(t):
            for b in blocks_of(t):
                total = k["q"][b].astype(F32)
                for i in range(z.n_snap - 1):
                    total = total + k["qr"][i, b].astype(F32)
                total = total.astype(BF16)
                k["own"][b] = total
                k["ext"][b] = total

        loop(z.tiles, tile)
        for d in range(z.lists):
            for t in range(z.list_len):
                k["snd"][d, t] = k["own"][ghosts[0, d, t]]

            @pl.when(inside(space - OFFSETS[d]))
            def _():
                ghost_copy(c, d).start()

            @pl.when(jnp.logical_not(inside(space + OFFSETS[d])))
            def _():
                first = z.rows + d * z.list_len
                k["ext"][first:first + z.list_len] = jnp.zeros((z.list_len, mc, bs), BF16)

        def gram(t, total):
            left = jnp.concatenate([k["own"][b] for b in blocks_of(t)], axis=1)
            return total + matmul(left, s["adjt"][columns(t), :])

        terms = lax.fori_loop(0, z.tiles, gram, jnp.zeros((mc, z.modes), F32)).T
        lane = sum_size + shift
        s["sum"][g]["d"][:, :, lane:lane + mc] = terms.astype(BF16).reshape(z.owners, z.piece, mc)

        for x, at, start, count in z.groups(first_mode, mc):
            @pl.when(snap == x)
            def _():
                def keep(t):
                    for b in blocks_of(t):
                        s["po"][at:at + count, pl.ds(pl.multiple_of(b * bs, bs), bs)] = k["own"][b, start:start + count, :]

                loop(z.tiles, keep)

    def terms_of(c):
        k = s["chunk"][c]
        first_mode, mc, g = z.parts[c]
        shift = first_mode - z.sums[g][0]
        for d in range(z.lists):
            @pl.when(inside(space + OFFSETS[d]))
            def _():
                ghost_copy(c, d).wait_recv()

        def tile(t, total):
            picked = [k["ext"][cols[j, b]] for b in blocks_of(t) for j in range(z.slots)]
            return total + matmul(jnp.concatenate(picked, axis=1), s["vt"][t])

        terms = lax.fori_loop(0, z.tiles, tile, jnp.zeros((mc, z.modes), F32)).T
        s["sum"][g]["d"][:, :, shift:shift + mc] = terms.astype(BF16).reshape(z.owners, z.piece, mc)

    def is_near(g):
        return g + 1 < len(z.sums)

    def targets(g):
        return [x for x, _, _, _ in z.groups(*z.sums[g])]

    def sum_of(g):
        k = s["sum"][g]
        slots = z.n_space if is_near(g) else z.devices
        settle(k["rs"], slots - 1, s["rs_r"].at[g])
        return lax.fori_loop(
            0,
            slots // 16,
            lambda i, t: t + jnp.sum(k["rs"][pl.ds(i * 16, 16)].astype(F32), axis=0),
            jnp.zeros((z.piece, 2 * z.sums[g][1]), F32),
        )

    def send_on(g):
        k = s["sum"][g]

        @pl.when(space < z.owners)
        def _():
            k["pt"][...] = sum_of(g)
            for x in targets(g):
                @pl.when(snap != x)
                def _():
                    pltpu.make_async_remote_copy(
                        src_ref=k["pt"],
                        dst_ref=k["ps"].at[lax.rem(snap - x + z.n_snap, z.n_snap) - 1],
                        send_sem=s["ps_s"].at[g],
                        recv_sem=s["ps_r"].at[g],
                        device_id=(space, x),
                        device_id_type=MESH,
                    ).start()

    def share_out(g):
        k = s["sum"][g]
        near = is_near(g)
        for x in [snap] if near else targets(g):
            def send(i):
                o = lax.rem(space + 1 + i, z.owners)
                slot = space if near else me
                same = (space == o) & (snap == x)

                @pl.when(same)
                def _():
                    k["rs"][slot] = k["d"][o]

                @pl.when(jnp.logical_not(same))
                def _():
                    pltpu.make_async_remote_copy(
                        src_ref=k["d"].at[o],
                        dst_ref=k["rs"].at[slot],
                        send_sem=s["rs_s"].at[g],
                        recv_sem=s["rs_r"].at[g],
                        device_id=(o, x),
                        device_id_type=MESH,
                    ).start()

            loop(z.owners, send)

    def apply(c, low, high):
        k = s["chunk"][c]
        for x, at, start, count in z.groups(*z.parts[c][:2]):
            @pl.when(snap == x)
            def _():
                def tile(t):
                    for b in blocks_of(low + t):
                        live = counts[b]
                        picked = []
                        for j in range(z.slots):
                            value = k["ext"][cols[j, b]][start:start + count]
                            picked.append(jnp.where(j < live, value, jnp.zeros_like(value)))
                        result = matmul(jnp.concatenate(picked, axis=1), s["opt"][b])
                        s["ao"][at:at + count, pl.ds(pl.multiple_of(b * bs, bs), bs)] = result.astype(BF16)

                loop(high - low, tile)

    def settle(ref, count, sem):
        part = ref.at[pl.ds(0, count)]
        pltpu.make_async_copy(part, part, sem).wait()

    def among(g):
        found = snap == z.groups(*z.sums[g])[0][0]
        for x, _, _, _ in z.groups(*z.sums[g])[1:]:
            found = found | (snap == x)
        return found

    def add_up(g):
        k = s["sum"][g]
        mc = z.sums[g][1]

        @pl.when(among(g) & (space < z.owners))
        def _():
            if is_near(g):
                total = k["pt"][...]
                settle(k["ps"], z.n_snap - 1, s["ps_r"].at[g])
                for i in range(z.n_snap - 1):
                    total = total + k["ps"][i]
            else:
                total = sum_of(g)
            total = (total * z.factor).astype(BF16)
            k["gs"][...] = total
            k["gat"][space] = total

            def send(i):
                pltpu.make_async_remote_copy(
                    src_ref=k["gs"],
                    dst_ref=k["gat"].at[space],
                    send_sem=s["ag_s"].at[g],
                    recv_sem=s["ag_r"].at[g],
                    device_id=(lax.rem(space + 1 + i, z.n_space), snap),
                    device_id_type=MESH,
                ).start()

            loop(z.n_space - 1, send)

    def finish(g):
        k = s["sum"][g]
        mc = z.sums[g][1]
        for x, at, start, count in z.groups(*z.sums[g]):
            @pl.when(snap == x)
            def _():
                @pl.when(space < z.owners)
                def _():
                    settle(k["gat"], z.owners - 1, s["ag_r"].at[g])

                if z.owners < z.n_space:
                    @pl.when(space >= z.owners)
                    def _():
                        settle(k["gat"], z.owners, s["ag_r"].at[g])

                whole = k["gat"][:z.owners].astype(F32).reshape(z.modes, 2 * mc)
                s["ro"][:, at:at + count] = whole[:, start:start + count]
                s["go"][:, at:at + count] = whole[:, mc + start:mc + start + count]

    loads[0].wait()
    s["cpt"][...] = transposed(s["cp"][...])
    loads[1].wait()
    for copy in loads[2:]:
        copy.start()
    project(0)
    pl.semaphore_wait(barrier, z.devices - 1)
    for h in range(2):
        for i in range(z.n_snap - 1):
            partial_copy(0, i, h).start()
    for c in range(1, z.chunks):
        project(c)

    loads[2].wait()
    cat = transposed(s["ca"][...])
    loads[3].wait()

    def adjoint(t):
        s["adjt"][columns(t), :] = matmul(cat, s["sa"][:, columns(t)]).T.astype(BF16)

    loop(z.tiles, adjoint)
    loads[4].wait()
    loop(z.tiles, carry_operator)

    stores = [
        pltpu.make_async_copy(s[name], target, s["store"].at[i])
        for i, (name, target) in enumerate(
            [("po", primal_out), ("ao", applied_out), ("ro", reduced_out), ("go", gram_out)]
        )
    ]
    last = z.chunks - 1

    def ends(c):
        return c == last or z.parts[c + 1][2] != z.parts[c][2]

    def reduced_terms(c):
        terms_of(c)
        if ends(c):
            share_out(z.parts[c][2])

    pending, passed = [], []
    for c in range(z.chunks):
        own_modes(c)
        if c == last:
            stores[0].start()
        for g in passed:
            add_up(g)
        for g in pending:
            send_on(g)
        passed, pending = pending, []
        if c:
            reduced_terms(c - 1)
            if ends(c - 1):
                pending = [z.parts[c - 1][2]]
            if c < last:
                apply(c - 1, 0, z.tiles)
    reduced_terms(last)
    for g in passed:
        add_up(g)
    apply(last - 1, 0, z.tiles)
    add_up(z.parts[last][2])
    apply(last, 0, z.tiles)
    stores[1].start()
    for g in range(len(z.sums)):
        finish(g)
    stores[2].start()
    stores[3].start()

    for c in range(z.chunks):
        for d in range(z.lists):
            @pl.when(inside(space - OFFSETS[d]))
            def _():
                ghost_copy(c, d).wait_send()

    for g in range(len(z.sums)):
        k = s["sum"][g]
        found = targets(g)
        owner = space < z.owners
        if is_near(g):
            @pl.when(owner)
            def _():
                settle(k["rs"], z.owners - 1, s["rs_s"].at[g])

                @pl.when(among(g))
                def _():
                    if len(found) > 1:
                        settle(k["ps"], len(found) - 1, s["ps_s"].at[g])

                @pl.when(jnp.logical_not(among(g)))
                def _():
                    settle(k["ps"], len(found), s["ps_s"].at[g])

            if z.owners < z.n_space:
                @pl.when(jnp.logical_not(owner))
                def _():
                    settle(k["rs"], z.owners, s["rs_s"].at[g])
        else:
            count = len(found) * z.owners

            @pl.when(owner & among(g))
            def _():
                settle(k["rs"], count - 1, s["rs_s"].at[g])

            @pl.when(jnp.logical_not(owner & among(g)))
            def _():
                settle(k["rs"], count, s["rs_s"].at[g])

        @pl.when(owner & among(g))
        def _():
            settle(k["gat"], z.n_space - 1, s["ag_s"].at[g])

    for copy in stores:
        copy.wait()


def hand_over(*refs):
    copies = [pltpu.make_async_copy(refs[i], refs[4 + i], refs[8].at[i]) for i in range(4)]
    for copy in copies:
        copy.start()
    for copy in copies:
        copy.wait()


def per_device(
    snaps_primal, snaps_adjoint, coef_primal, coef_adjoint, op_blocks, counts, col_index, ghost_send
):
    z = Sizes(
        lax.axis_size("space"), lax.axis_size("snap"), snaps_primal, coef_primal, op_blocks, ghost_send
    )
    any_spec = pl.BlockSpec(memory_space=pl.ANY)
    smem = pl.BlockSpec(memory_space=pltpu.SMEM)
    names = scratch_of(z)
    flat, tree = jax.tree.flatten(names)

    def body(*refs):
        s = jax.tree.unflatten(tree, refs[12:])
        kernel(z, *refs[:12], s)

    flops = 2 * z.unknowns * z.modes * (2 * z.snaps + z.slots * z.bs + 2 * z.modes)
    shapes = (
        jax.ShapeDtypeStruct((z.share, z.unknowns), BF16),
        jax.ShapeDtypeStruct((z.share, z.unknowns), BF16),
        jax.ShapeDtypeStruct((z.modes, z.share), F32),
        jax.ShapeDtypeStruct((z.modes, z.share), F32),
    )
    results = pl.pallas_call(
        body,
        out_shape=shapes,
        in_specs=[any_spec] * 5 + [smem] * 3,
        out_specs=[any_spec] * 4,
        scratch_shapes=flat,
        cost_estimate=pl.CostEstimate(flops=flops, bytes_accessed=10_000_000, transcendentals=0),
        compiler_params=pltpu.CompilerParams(
            collective_id=0, has_side_effects=True, vmem_limit_bytes=58 * 1024 * 1024
        ),
    )(snaps_primal, snaps_adjoint, coef_primal, coef_adjoint, op_blocks, counts, col_index.T, ghost_send)
    return pl.pallas_call(
        hand_over,
        out_shape=shapes,
        in_specs=[pl.BlockSpec(memory_space=pltpu.VMEM)] * 4,
        out_specs=[any_spec] * 4,
        scratch_shapes=[pltpu.SemaphoreType.DMA((4,))],
    )(*results)


def solution(mesh):
    placed = (
        P("snap", "space"),
        P("snap", "space"),
        P("snap", None),
        P("snap", None),
        P("space", None, None, None),
        P("space"),
        P("space", None),
        P("space", None, None),
    )
    return jax.shard_map(
        per_device,
        mesh=mesh,
        in_specs=placed,
        out_specs=(P("snap", "space"), P("snap", "space"), P(None, "snap"), P(None, "snap")),
        check_vma=False,
    )
```

```python
import math

import jax
import jax.numpy as jnp
from jax import lax
from jax.experimental import pallas as pl
from jax.experimental.pallas import tpu as pltpu
from jax.sharding import PartitionSpec as P

MESH = pl.DeviceIdType.MESH
BF16 = jnp.bfloat16
F32 = jnp.float32
OFFSETS = (-2, -1, 1, 2)
TILE_BLOCKS = 4
CHUNKS = ((64,), (64,), (64,), (32, 32))


class Sizes:
    def __init__(self, n_space, n_snap, snaps, coef, op_blocks, ghost_send):
        self.n_space, self.n_snap = n_space, n_snap
        self.devices = n_space * n_snap
        self.snaps, self.unknowns = snaps.shape
        self.modes = coef.shape[1]
        self.share = self.modes // n_snap
        self.rows, self.slots, self.bs = op_blocks.shape[:3]
        self.lists, self.list_len = ghost_send.shape[1:]
        self.parts, self.sums, first = [], [], 0
        for g, sizes in enumerate(CHUNKS):
            self.sums.append((first, sum(sizes)))
            for size in sizes:
                self.parts.append((first, size, g))
                first += size
        assert first == self.modes
        self.chunks = len(self.parts)
        self.piece = max(16, self.modes // n_space)
        self.owners = self.modes // self.piece
        self.tiles = self.rows // TILE_BLOCKS
        self.factor = 1.0 / math.sqrt(self.unknowns * n_space)

    def groups(self, first, size):
        last = first + size
        found = []
        for x in range(self.n_snap):
            lo, hi = max(first, x * self.share), min(last, (x + 1) * self.share)
            if lo < hi:
                found.append((x, lo - x * self.share, lo - first, hi - lo))
        return found


def chunk_scratch(z, mc):
    b, bs = z.rows, z.bs
    return {
        "q": pltpu.VMEM((b, mc, bs), BF16),
        "qr": pltpu.VMEM((z.n_snap - 1, b, mc, bs), BF16),
        "own": pltpu.VMEM((b, mc, bs), BF16),
        "ext": pltpu.VMEM((b + z.lists * z.list_len, mc, bs), BF16),
        "snd": pltpu.VMEM((z.lists, z.list_len, mc, bs), BF16),
    }


def sum_scratch(z, mc, near):
    return {
        "pt": pltpu.VMEM((z.piece, 2 * mc), F32),
        "ps": pltpu.VMEM((z.n_snap - 1, z.piece, 2 * mc), F32),
        "d": pltpu.VMEM((z.owners, z.piece, 2 * mc), BF16),
        "rs": pltpu.VMEM((z.n_space if near else z.devices, z.piece, 2 * mc), BF16),
        "gs": pltpu.VMEM((z.piece, 2 * mc), BF16),
        "gat": pltpu.VMEM((z.n_space, z.piece, 2 * mc), BF16),
    }


def scratch_of(z):
    bs = z.bs
    sem = pltpu.SemaphoreType.DMA
    return {
        "sp": pltpu.VMEM((z.snaps, z.unknowns), BF16),
        "sa": pltpu.VMEM((z.snaps, z.unknowns), BF16),
        "cp": pltpu.VMEM((z.snaps, z.modes), BF16),
        "ca": pltpu.VMEM((z.snaps, z.modes), BF16),
        "op": pltpu.VMEM((z.rows, z.slots, bs, bs), BF16),
        "adjt": pltpu.VMEM((z.unknowns, z.modes), BF16),
        "opt": pltpu.VMEM((z.rows, z.slots * bs, bs), BF16),
        "vt": pltpu.VMEM((z.tiles, TILE_BLOCKS * z.slots * bs, z.modes), BF16),
        "po": pltpu.VMEM((z.share, z.unknowns), BF16),
        "ao": pltpu.VMEM((z.share, z.unknowns), BF16),
        "ro": pltpu.VMEM((z.modes, z.share), F32),
        "go": pltpu.VMEM((z.modes, z.share), F32),
        "store": sem((4,)),
        "cpt": pltpu.VMEM((z.modes, z.snaps), BF16),
        "load": sem((5,)),
        "q_s": sem((z.chunks, z.n_snap - 1, 2)),
        "q_r": sem((z.chunks, z.n_snap - 1, 2)),
        "g_s": sem((z.chunks, z.lists)),
        "g_r": sem((z.chunks, z.lists)),
        "rs_s": sem((len(z.sums),)),
        "rs_r": sem((len(z.sums),)),
        "ps_s": sem((len(z.sums),)),
        "ps_r": sem((len(z.sums),)),
        "ag_s": sem((len(z.sums),)),
        "ag_r": sem((len(z.sums),)),
        "chunk": [chunk_scratch(z, size) for _, size, _ in z.parts],
        "sum": [sum_scratch(z, size, g + 1 < len(z.sums)) for g, (_, size) in enumerate(z.sums)],
    }


def transposed(value):
    return value.astype(F32).T.astype(BF16)


def matmul(a, b):
    return jnp.dot(a, b, preferred_element_type=F32)


def loop(count, body):
    def step(i, carry):
        body(i)
        return carry

    lax.fori_loop(0, count, step, 0)


def kernel(z, sp_hbm, sa_hbm, cp_hbm, ca_hbm, op_hbm, counts, cols, ghosts,
           primal_out, applied_out, reduced_out, gram_out, s):
    space, snap = lax.axis_index("space"), lax.axis_index("snap")
    me = space * z.n_snap + snap
    bs = z.bs
    width = TILE_BLOCKS * bs

    loads = [
        pltpu.make_async_copy(source, s[name], s["load"].at[i])
        for i, (source, name) in enumerate(
            [(cp_hbm, "cp"), (sp_hbm, "sp"), (ca_hbm, "ca"), (sa_hbm, "sa"), (op_hbm, "op")]
        )
    ]
    for copy in loads[:2]:
        copy.start()

    barrier = pltpu.get_barrier_semaphore()

    def greet(i):
        other = lax.rem(me + 1 + i, z.devices)
        pl.semaphore_signal(
            barrier,
            inc=1,
            device_id=(lax.div(other, z.n_snap), lax.rem(other, z.n_snap)),
            device_id_type=MESH,
        )

    loop(z.devices - 1, greet)

    def columns(t):
        return pl.ds(pl.multiple_of(t * width, width), width)

    def project(c):
        first, mc, _ = z.parts[c]
        coef = s["cpt"][first:first + mc, :]
        q = s["chunk"][c]["q"]

        def tile(t):
            part = jnp.dot(coef, s["sp"][:, columns(t)], preferred_element_type=F32).astype(BF16)
            for i in range(TILE_BLOCKS):
                q[t * TILE_BLOCKS + i] = part[:, i * bs:(i + 1) * bs]

        loop(z.tiles, tile)

    def partial_copy(c, i, h):
        k = s["chunk"][c]
        half = z.rows // 2
        return pltpu.make_async_remote_copy(
            src_ref=k["q"].at[pl.ds(h * half, half)],
            dst_ref=k["qr"].at[i, pl.ds(h * half, half)],
            send_sem=s["q_s"].at[c, i, h],
            recv_sem=s["q_r"].at[c, i, h],
            device_id=(space, lax.rem(snap + 1 + i, z.n_snap)),
            device_id_type=MESH,
        )

    def ghost_copy(c, d):
        k = s["chunk"][c]
        first = z.rows + d * z.list_len
        return pltpu.make_async_remote_copy(
            src_ref=k["snd"].at[d],
            dst_ref=k["ext"].at[pl.ds(first, z.list_len)],
            send_sem=s["g_s"].at[c, d],
            recv_sem=s["g_r"].at[c, d],
            device_id=(space - OFFSETS[d], snap),
            device_id_type=MESH,
        )

    def inside(position):
        return (position >= 0) & (position < z.n_space)

    def blocks_of(t):
        return [t * TILE_BLOCKS + i for i in range(TILE_BLOCKS)]

    def carry_operator(t):
        for i, b in enumerate(blocks_of(t)):
            live = counts[b]
            for j in range(z.slots):
                s["opt"][b, j * bs:(j + 1) * bs, :] = s["op"][b, j].T
            part = matmul(s["opt"][b], s["adjt"][pl.ds(pl.multiple_of(b * bs, bs), bs), :])
            for j in range(z.slots):
                value = part[j * bs:(j + 1) * bs]
                value = jnp.where(j < live, value, jnp.zeros_like(value)).astype(BF16)
                first = (i * z.slots + j) * bs
                s["vt"][t, first:first + bs, :] = value

    def own_modes(c):
        k = s["chunk"][c]
        first_mode, mc, g = z.parts[c]
        sum_first, sum_size = z.sums[g]
        shift = first_mode - sum_first
        for h in range(2):
            for i in range(z.n_snap - 1):
                partial_copy(c, i, h).wait()
                if c + 1 + h < z.chunks:
                    partial_copy(c + 1 + h, i, 1 - h).start()

        def tile(t):
            for b in blocks_of(t):
                total = k["q"][b].astype(F32)
                for i in range(z.n_snap - 1):
                    total = total + k["qr"][i, b].astype(F32)
                total = total.astype(BF16)
                k["own"][b] = total
                k["ext"][b] = total

        loop(z.tiles, tile)
        for d in range(z.lists):
            for t in range(z.list_len):
                k["snd"][d, t] = k["own"][ghosts[0, d, t]]

            @pl.when(inside(space - OFFSETS[d]))
            def _():
                ghost_copy(c, d).start()

            @pl.when(jnp.logical_not(inside(space + OFFSETS[d])))
            def _():
                first = z.rows + d * z.list_len
                k["ext"][first:first + z.list_len] = jnp.zeros((z.list_len, mc, bs), BF16)

        def gram(t, total):
            left = jnp.concatenate([k["own"][b] for b in blocks_of(t)], axis=1)
            return total + matmul(left, s["adjt"][columns(t), :])

        terms = lax.fori_loop(0, z.tiles, gram, jnp.zeros((mc, z.modes), F32)).T
        lane = sum_size + shift
        s["sum"][g]["d"][:, :, lane:lane + mc] = terms.astype(BF16).reshape(z.owners, z.piece, mc)

        for x, at, start, count in z.groups(first_mode, mc):
            @pl.when(snap == x)
            def _():
                def keep(t):
                    for b in blocks_of(t):
                        s["po"][at:at + count, pl.ds(pl.multiple_of(b * bs, bs), bs)] = k["own"][b, start:start + count, :]

                loop(z.tiles, keep)

    def terms_of(c):
        k = s["chunk"][c]
        first_mode, mc, g = z.parts[c]
        shift = first_mode - z.sums[g][0]
        for d in range(z.lists):
            @pl.when(inside(space + OFFSETS[d]))
            def _():
                ghost_copy(c, d).wait_recv()

        def tile(t, total):
            picked = [k["ext"][cols[j, b]] for b in blocks_of(t) for j in range(z.slots)]
            return total + matmul(jnp.concatenate(picked, axis=1), s["vt"][t])

        terms = lax.fori_loop(0, z.tiles, tile, jnp.zeros((mc, z.modes), F32)).T
        s["sum"][g]["d"][:, :, shift:shift + mc] = terms.astype(BF16).reshape(z.owners, z.piece, mc)

    def is_near(g):
        return g + 1 < len(z.sums)

    def targets(g):
        return [x for x, _, _, _ in z.groups(*z.sums[g])]

    def sum_of(g):
        k = s["sum"][g]
        slots = z.n_space if is_near(g) else z.devices
        settle(k["rs"], slots - 1, s["rs_r"].at[g])
        return lax.fori_loop(
            0,
            slots // 16,
            lambda i, t: t + jnp.sum(k["rs"][pl.ds(i * 16, 16)].astype(F32), axis=0),
            jnp.zeros((z.piece, 2 * z.sums[g][1]), F32),
        )

    def send_on(g):
        k = s["sum"][g]

        @pl.when(space < z.owners)
        def _():
            k["pt"][...] = sum_of(g)
            for x in targets(g):
                @pl.when(snap != x)
                def _():
                    pltpu.make_async_remote_copy(
                        src_ref=k["pt"],
                        dst_ref=k["ps"].at[lax.rem(snap - x + z.n_snap, z.n_snap) - 1],
                        send_sem=s["ps_s"].at[g],
                        recv_sem=s["ps_r"].at[g],
                        device_id=(space, x),
                        device_id_type=MESH,
                    ).start()

    def share_out(g):
        k = s["sum"][g]
        near = is_near(g)
        for x in [snap] if near else targets(g):
            def send(i):
                o = lax.rem(space + 1 + i, z.owners)
                slot = space if near else me
                same = (space == o) & (snap == x)

                @pl.when(same)
                def _():
                    k["rs"][slot] = k["d"][o]

                @pl.when(jnp.logical_not(same))
                def _():
                    pltpu.make_async_remote_copy(
                        src_ref=k["d"].at[o],
                        dst_ref=k["rs"].at[slot],
                        send_sem=s["rs_s"].at[g],
                        recv_sem=s["rs_r"].at[g],
                        device_id=(o, x),
                        device_id_type=MESH,
                    ).start()

            loop(z.owners, send)

    def apply(c, low, high):
        k = s["chunk"][c]
        for x, at, start, count in z.groups(*z.parts[c][:2]):
            @pl.when(snap == x)
            def _():
                def tile(t):
                    for b in blocks_of(low + t):
                        live = counts[b]
                        picked = []
                        for j in range(z.slots):
                            value = k["ext"][cols[j, b]][start:start + count]
                            picked.append(jnp.where(j < live, value, jnp.zeros_like(value)))
                        result = matmul(jnp.concatenate(picked, axis=1), s["opt"][b])
                        s["ao"][at:at + count, pl.ds(pl.multiple_of(b * bs, bs), bs)] = result.astype(BF16)

                loop(high - low, tile)

    def settle(ref, count, sem):
        part = ref.at[pl.ds(0, count)]
        pltpu.make_async_copy(part, part, sem).wait()

    def among(g):
        found = snap == z.groups(*z.sums[g])[0][0]
        for x, _, _, _ in z.groups(*z.sums[g])[1:]:
            found = found | (snap == x)
        return found

    def add_up(g):
        k = s["sum"][g]
        mc = z.sums[g][1]

        @pl.when(among(g) & (space < z.owners))
        def _():
            if is_near(g):
                total = k["pt"][...]
                settle(k["ps"], z.n_snap - 1, s["ps_r"].at[g])
                for i in range(z.n_snap - 1):
                    total = total + k["ps"][i]
            else:
                total = sum_of(g)
            total = (total * z.factor).astype(BF16)
            k["gs"][...] = total
            k["gat"][space] = total

            def send(i):
                pltpu.make_async_remote_copy(
                    src_ref=k["gs"],
                    dst_ref=k["gat"].at[space],
                    send_sem=s["ag_s"].at[g],
                    recv_sem=s["ag_r"].at[g],
                    device_id=(lax.rem(space + 1 + i, z.n_space), snap),
                    device_id_type=MESH,
                ).start()

            loop(z.n_space - 1, send)

    def finish(g):
        k = s["sum"][g]
        mc = z.sums[g][1]
        for x, at, start, count in z.groups(*z.sums[g]):
            @pl.when(snap == x)
            def _():
                @pl.when(space < z.owners)
                def _():
                    settle(k["gat"], z.owners - 1, s["ag_r"].at[g])

                if z.owners < z.n_space:
                    @pl.when(space >= z.owners)
                    def _():
                        settle(k["gat"], z.owners, s["ag_r"].at[g])

                whole = k["gat"][:z.owners].astype(F32).reshape(z.modes, 2 * mc)
                s["ro"][:, at:at + count] = whole[:, start:start + count]
                s["go"][:, at:at + count] = whole[:, mc + start:mc + start + count]

    loads[0].wait()
    s["cpt"][...] = transposed(s["cp"][...])
    loads[1].wait()
    for copy in loads[2:]:
        copy.start()
    project(0)
    pl.semaphore_wait(barrier, z.devices - 1)
    for h in range(2):
        for i in range(z.n_snap - 1):
            partial_copy(0, i, h).start()
    for c in range(1, z.chunks):
        project(c)
        if c == 1:
            for i in range(z.n_snap - 1):
                partial_copy(1, i, 0).start()

    loads[2].wait()
    cat = transposed(s["ca"][...])
    loads[3].wait()

    def adjoint(t):
        s["adjt"][columns(t), :] = matmul(cat, s["sa"][:, columns(t)]).T.astype(BF16)

    loop(z.tiles, adjoint)
    loads[4].wait()
    loop(z.tiles, carry_operator)

    stores = [
        pltpu.make_async_copy(s[name], target, s["store"].at[i])
        for i, (name, target) in enumerate(
            [("po", primal_out), ("ao", applied_out), ("ro", reduced_out), ("go", gram_out)]
        )
    ]
    last = z.chunks - 1

    def ends(c):
        return c == last or z.parts[c + 1][2] != z.parts[c][2]

    def reduced_terms(c):
        terms_of(c)
        if ends(c):
            share_out(z.parts[c][2])

    pending, passed = [], []
    for c in range(z.chunks):
        own_modes(c)
        if c == last:
            stores[0].start()
        for g in passed:
            add_up(g)
        for g in pending:
            send_on(g)
        passed, pending = pending, []
        if c:
            reduced_terms(c - 1)
            if ends(c - 1):
                pending = [z.parts[c - 1][2]]
            if c < last:
                apply(c - 1, 0, z.tiles)
    reduced_terms(last)
    for g in passed:
        add_up(g)
    apply(last - 1, 0, z.tiles)
    add_up(z.parts[last][2])
    apply(last, 0, z.tiles)
    stores[1].start()
    for g in range(len(z.sums)):
        finish(g)
    stores[2].start()
    stores[3].start()

    for c in range(z.chunks):
        for d in range(z.lists):
            @pl.when(inside(space - OFFSETS[d]))
            def _():
                ghost_copy(c, d).wait_send()

    for g in range(len(z.sums)):
        k = s["sum"][g]
        found = targets(g)
        owner = space < z.owners
        if is_near(g):
            @pl.when(owner)
            def _():
                settle(k["rs"], z.owners - 1, s["rs_s"].at[g])

                @pl.when(among(g))
                def _():
                    if len(found) > 1:
                        settle(k["ps"], len(found) - 1, s["ps_s"].at[g])

                @pl.when(jnp.logical_not(among(g)))
                def _():
                    settle(k["ps"], len(found), s["ps_s"].at[g])

            if z.owners < z.n_space:
                @pl.when(jnp.logical_not(owner))
                def _():
                    settle(k["rs"], z.owners, s["rs_s"].at[g])
        else:
            count = len(found) * z.owners

            @pl.when(owner & among(g))
            def _():
                settle(k["rs"], count - 1, s["rs_s"].at[g])

            @pl.when(jnp.logical_not(owner & among(g)))
            def _():
                settle(k["rs"], count, s["rs_s"].at[g])

        @pl.when(owner & among(g))
        def _():
            settle(k["gat"], z.n_space - 1, s["ag_s"].at[g])

    for copy in stores:
        copy.wait()


def hand_over(*refs):
    copies = [pltpu.make_async_copy(refs[i], refs[4 + i], refs[8].at[i]) for i in range(4)]
    for copy in copies:
        copy.start()
    for copy in copies:
        copy.wait()


def per_device(
    snaps_primal, snaps_adjoint, coef_primal, coef_adjoint, op_blocks, counts, col_index, ghost_send
):
    z = Sizes(
        lax.axis_size("space"), lax.axis_size("snap"), snaps_primal, coef_primal, op_blocks, ghost_send
    )
    any_spec = pl.BlockSpec(memory_space=pl.ANY)
    smem = pl.BlockSpec(memory_space=pltpu.SMEM)
    names = scratch_of(z)
    flat, tree = jax.tree.flatten(names)

    def body(*refs):
        s = jax.tree.unflatten(tree, refs[12:])
        kernel(z, *refs[:12], s)

    flops = 2 * z.unknowns * z.modes * (2 * z.snaps + z.slots * z.bs + 2 * z.modes)
    shapes = (
        jax.ShapeDtypeStruct((z.share, z.unknowns), BF16),
        jax.ShapeDtypeStruct((z.share, z.unknowns), BF16),
        jax.ShapeDtypeStruct((z.modes, z.share), F32),
        jax.ShapeDtypeStruct((z.modes, z.share), F32),
    )
    results = pl.pallas_call(
        body,
        out_shape=shapes,
        in_specs=[any_spec] * 5 + [smem] * 3,
        out_specs=[any_spec] * 4,
        scratch_shapes=flat,
        cost_estimate=pl.CostEstimate(flops=flops, bytes_accessed=10_000_000, transcendentals=0),
        compiler_params=pltpu.CompilerParams(
            collective_id=0, has_side_effects=True, vmem_limit_bytes=58 * 1024 * 1024
        ),
    )(snaps_primal, snaps_adjoint, coef_primal, coef_adjoint, op_blocks, counts, col_index.T, ghost_send)
    return pl.pallas_call(
        hand_over,
        out_shape=shapes,
        in_specs=[pl.BlockSpec(memory_space=pltpu.VMEM)] * 4,
        out_specs=[any_spec] * 4,
        scratch_shapes=[pltpu.SemaphoreType.DMA((4,))],
    )(*results)


def solution(mesh):
    placed = (
        P("snap", "space"),
        P("snap", "space"),
        P("snap", None),
        P("snap", None),
        P("space", None, None, None),
        P("space"),
        P("space", None),
        P("space", None, None),
    )
    return jax.shard_map(
        per_device,
        mesh=mesh,
        in_specs=placed,
        out_specs=(P("snap", "space"), P("snap", "space"), P(None, "snap"), P(None, "snap")),
        check_vma=False,
    )
```
